32 devices in a mesh: node: 16 (over z, y, x), rel: 2 (over core).
Axes of the slice: x: 2, y: 2, z: 4, core: 2. Of those that a mesh axis runs over, the one named last changes fastest.
Arguments:
- features: bfloat16 [8192, 768], P('node'), may hold values from -6 to 6
- history: bfloat16 [8192, 768], P('node'), may hold values from -6 to 6
- history_mean: bfloat16 [6, 4096, 768], P('rel', 'node'), may hold values from -6 to 6
- weights: bfloat16 [6, 768, 768], P('rel'), may hold values from -0.09375 to 0.09375
- source_rows: int32 [6, 8192], P('rel', 'node'), may hold values from 0 to 511
- target_owner: int32 [6, 8192, 1], P('rel', 'node'), may hold values from 0 to 15; in each aligned block of 512 rows (0 to 511, 512 to 1023, ..., all dimensions but the last counted through in order) at most 80 rows name the same one
- target_rows: int32 [6, 8192], P('rel', 'node'), may hold values from 0 to 255
- cotangent: bfloat16 [4096, 768], P('node'), may hold values from -6 to 6
Outputs:
- layer_out: bfloat16 [4096, 768], P('node')
- weight_grads: float32 [6, 768, 768], P('rel')
- feature_grads: bfloat16 [8192, 768], P('node')
The draws below stay inside these ranges and needn't reach their ends.
Inputs may be any that keep to these rules, and one draw needn't show every extreme that they name: `target_owner`: within each relation, among the 512 edges of one owner's aligned block, at most 80 name the same target owner, and some target owner is named by exactly 80 of them.
All inputs are finite; a program needn't handle non-finite values.
Results may differ from the reference program's by a relative error of at most 0.0055.
Values may be sent and summed in bfloat16 or wider, within the bound.
No kernel may reach another device: no remote copies, remote signals or barrier semaphores. Data moves between devices by JAX's collectives and lax.ppermute only.
A program may use at most 128 MiB of HBM per device.

```python
import math
import jax
import jax.numpy as jnp
import numpy as np

D = 768
RELS = 6
SAMPLES = 2
B_DEV = 256
NODE_DEV = 512
MSG_DEV = 512
CAP = 80
BATCH = 4096
NODES = 8192
MSG_TOTAL = 8192
N_NODE = 16


def touch_ends(drawn, stream_key, least, largest):
    spot = [jax.random.randint(jax.random.fold_in(stream_key, axis), (), 0, length) for axis, length in enumerate(drawn.shape)]
    main_axis = drawn.shape.index(max(drawn.shape))
    neighbour = spot[:main_axis] + [(spot[main_axis] + 1) % drawn.shape[main_axis]] + spot[main_axis + 1:]
    return drawn.at[tuple(spot)].set(least).at[tuple(neighbour)].set(largest)


def block_scale(rng, extent, shards, low, top_value):
    factor_of, own = 1.0, jax.random.fold_in(rng, 6)
    for dim, shards_of in shards:
        heights = jnp.exp(jax.random.uniform(jax.random.fold_in(own, dim), (shards_of,), jnp.float32, low / len(shards), top_value / len(shards)))
        factor_of = factor_of * jnp.repeat(heights, extent[dim] // shards_of).reshape([-1 if axis == dim else 1 for axis in range(len(extent))])
    return factor_of


def shared_out(rng, own, number, rows, number_of, top, limit, lean):
    sequence = jax.random.permutation(rng, number_of)
    crowded, usual = load_shares(number_of, rows * top, limit, lean, True), load_shares(number_of, rows * top, limit, lean, False)
    places = jnp.arange(number_of)

    def named(lengths, offset_by):
        used = int((lengths > 0).sum())
        fixed = max(1, used // 4)
        passed = fixed + (places - fixed + offset_by * (used - fixed)) % max(1, number_of - fixed)
        return jnp.zeros((number_of,), jnp.int32).at[sequence[jnp.where(places < fixed, places, passed)]].set(jnp.asarray(lengths, jnp.int32))

    lengths = jnp.where(number % 4 == 0, named(crowded, number // 4), named(usual, number - number // 4 - 1))
    mixed = jax.random.permutation(jax.random.fold_in(own, 3), number_of)
    donor, receiver = mixed[0:number_of // 2 * 2:2], mixed[1:number_of // 2 * 2:2]
    margin = jnp.minimum(lengths[donor] - 1, limit - lengths[receiver]) // 2
    margin = jnp.where((donor == sequence[0]) | (receiver == sequence[0]) | (lengths[receiver] == 0), 0, jnp.maximum(margin, 0))
    passed = jax.random.randint(jax.random.fold_in(own, 4), (number_of // 2,), 0, 1 << 20) % (margin + 1)
    lengths = lengths.at[donor].add(-passed).at[receiver].add(passed)
    members = jnp.searchsorted(jnp.cumsum(lengths), jnp.arange(rows * top), side="right").astype(jnp.int32)
    table = members.reshape(top, rows).T
    table = table[jax.random.permutation(jax.random.fold_in(own, 1), rows)]
    offset_by = jax.random.randint(jax.random.fold_in(own, 2), (rows, 1), 0, top)
    return jnp.take_along_axis(table, (jnp.arange(top)[None, :] + offset_by) % top, axis=1)


def load_shares(count, total, reach, slope, full):
    loads = [(1 << 20) // math.isqrt(rank ** slope) + 1 for rank in range(1, count + 1)]
    largest = reach if full else min(reach, max(-(-total // count), total * loads[0] // sum(loads)))
    least = 1 if total - largest >= count - 1 else 0
    holding, spare = [largest] + [least] * (count - 1), total - largest - least * (count - 1)
    while spare > 0:
        free = [i for i in range(1, count) if holding[i] < largest] or [i for i in range(1, count) if holding[i] < reach]
        whole, left = sum([loads[i] for i in free]), spare
        for i in free:
            addition = min(reach - holding[i], max(1, left * loads[i] // whole), spare)
            holding[i] = holding[i] + addition
            spare = spare - addition
    return np.array(holding)


def centred(rng, extent, scale, reach, pieces=(), dtype=jnp.bfloat16):
    result = jax.random.normal(rng, extent, jnp.float32) * scale
    if len(pieces) > 0:
        result = block_scale(rng, extent, pieces, -0.22, 0.18) * result
    return jnp.clip(result, min=-reach, max=reach).astype(dtype)


def setup_inputs(seed: int = 0) -> dict:
    key_of = jax.random.split(jax.random.key(seed), 9)
    features = centred(key_of[0], (NODES, D), 1.0, 6.0, ((0, 16),))
    history = centred(key_of[1], (NODES, D), 1.0, 6.0, ((0, 16),))
    history_mean = centred(key_of[2], (RELS, BATCH, D), 1.0, 6.0, ((0, 2), (1, 16)))
    weights = centred(key_of[3], (RELS, D, D), (D * RELS) ** -0.5, 0.09375, ((0, 2),))
    source_rows = touch_ends(jax.random.randint(key_of[4], (RELS, MSG_TOTAL), 0, NODE_DEV), jax.random.fold_in(key_of[4], 1), 0, NODE_DEV - 1).astype(jnp.int32)
    target_owner_keys = jax.random.split(jax.random.fold_in(key_of[5], 1), RELS * MSG_TOTAL // MSG_DEV)
    target_owner_turns = jax.random.permutation(jax.random.fold_in(key_of[5], 3), RELS * MSG_TOTAL // MSG_DEV)
    target_owner = jax.vmap(lambda own, number: shared_out(jax.random.fold_in(key_of[5], 2), own, number, MSG_DEV, N_NODE, 1, CAP, 1))(target_owner_keys, target_owner_turns).reshape((RELS, MSG_TOTAL, 1))
    target_rows = touch_ends(jax.random.randint(key_of[6], (RELS, MSG_TOTAL), 0, B_DEV), jax.random.fold_in(key_of[6], 1), 0, B_DEV - 1).astype(jnp.int32)
    cotangent = centred(key_of[7], (BATCH, D), 1.0, 6.0, ((0, 16),))
    return dict(features=features, history=history, history_mean=history_mean, weights=weights, source_rows=source_rows, target_owner=target_owner, target_rows=target_rows, cotangent=cotangent)


def reference(features, history, history_mean, weights, source_rows, target_owner, target_rows, cotangent):
    deltas = (features.astype(jnp.float32) - history.astype(jnp.float32)).astype(jnp.bfloat16)
    owner_of = (jnp.arange(MSG_TOTAL) // MSG_DEV).astype(jnp.int32)
    total = jnp.zeros((BATCH, D), jnp.float32)
    grads = []
    back = jnp.zeros((NODES, D), jnp.float32)
    scale = 1.0 / SAMPLES
    for rel_id in range(RELS):
        src = (owner_of * NODE_DEV + source_rows[rel_id]).astype(jnp.int32)
        dst = (target_owner[rel_id, :, 0] * B_DEV + target_rows[rel_id]).astype(jnp.int32)
        moved = jnp.take(deltas, src, axis=0).astype(jnp.float32)
        summed = jax.ops.segment_sum(moved, dst, num_segments=BATCH)
        aggregate = (history_mean[rel_id].astype(jnp.float32) + scale * summed).astype(jnp.bfloat16)
        total = total + jnp.dot(aggregate, weights[rel_id], preferred_element_type=jnp.float32)
        grads.append(jnp.dot(aggregate.T, cotangent, preferred_element_type=jnp.float32) / jnp.sqrt(jnp.float32(BATCH)))
        edge_grads = (scale * jnp.dot(cotangent, weights[rel_id].T, preferred_element_type=jnp.float32)).astype(jnp.bfloat16)
        carried = jnp.take(edge_grads, dst, axis=0).astype(jnp.float32)
        back = back + jax.ops.segment_sum(carried, src, num_segments=NODES)
    return (total.astype(jnp.bfloat16), jnp.stack(grads), back.astype(jnp.bfloat16))
```

```python
import functools

import jax
import jax.numpy as jnp
from jax import lax
from jax.experimental import pallas as pl
from jax.experimental.pallas import tpu as pltpu
from jax.sharding import PartitionSpec as P

BF = jnp.bfloat16
F32 = jnp.float32
AXES = ("node", "rel")
DEPTH, SIDE = 4, 2
NODES_HERE = DEPTH * SIDE * SIDE


def dot(a, b, dims=((1,), (0,))):
    return lax.dot_general(a, b, (dims, ((), ())), preferred_element_type=F32)


def cost(flops, moved):
    return pl.CostEstimate(flops=int(flops), bytes_accessed=int(moved), transcendentals=0)


def params(steps=1):
    return pltpu.CompilerParams(
        dimension_semantics=("arbitrary",) * steps, vmem_limit_bytes=48 * 1024 * 1024
    )


def pairs(move):
    listed = []
    for node in range(NODES_HERE):
        for core in range(2):
            z, y, x = node // 4, node // 2 % 2, node % 2
            tz, ty, tx, tc = move(z, y, x, core)
            listed.append((node * 2 + core, (tz * 4 + ty * 2 + tx) * 2 + tc))
    return listed


FIRST = pairs(lambda z, y, x, c: (z, y ^ (1 - c), x ^ c, c))
SECOND = pairs(lambda z, y, x, c: (z, y ^ c, x ^ (1 - c), c))
ALONG = [pairs(lambda z, y, x, c, k=k: ((z + k) % DEPTH, y, x, c)) for k in range(DEPTH)]
CORES = pairs(lambda z, y, x, c: (z, y, x, 1 - c))


def hop(array, table):
    return lax.ppermute(array, AXES, table)


def owner_of(pos_ref, core, first, second, depth):
    z, y, x = pos_ref[0], pos_ref[1], pos_ref[2]
    flip_y = jnp.where(core == 0, first, second)
    flip_x = jnp.where(core == 0, second, first)
    y = y + flip_y - 2 * y * flip_y
    x = x + flip_x - 2 * x * flip_x
    return lax.rem(z + depth + DEPTH, DEPTH) * 4 + y * 2 + x


def edges_kernel(scale, feat, hist, mean, weight, src, dst, moved, sent, spread, local):
    step = pl.program_id(0)
    nodes, msgs = feat.shape[0], src.shape[2]
    deltas = (feat[...].astype(F32) - hist[...].astype(F32)).astype(BF)
    column = jnp.transpose(jnp.broadcast_to(src[0], (128, msgs)))
    lanes = lax.broadcasted_iota(jnp.int32, (msgs, 128), 1)
    hot = jnp.concatenate(
        [(column == lanes + n).astype(F32).astype(BF) for n in range(0, nodes, 128)], axis=1
    )
    rows = dot(hot, deltas).astype(BF)
    moved[0] = rows
    sent[0] = (scale * dot(rows, weight[0])).astype(BF)
    spread[0] = jnp.transpose(jnp.broadcast_to(dst[0], (128, msgs)))
    own = dot(mean[0], weight[0])

    @pl.when(step == 0)
    def _():
        local[...] = own

    @pl.when(step > 0)
    def _():
        local[...] += own


def edges(features, history, mean, weights, src, dst, scale):
    groups, width, _ = weights.shape
    nodes, batch, msgs = features.shape[0], mean.shape[1], src.shape[2]
    whole = lambda *shape: pl.BlockSpec(shape, lambda r: (0,) * len(shape))
    by_rel = lambda *shape: pl.BlockSpec((1,) + shape, lambda r: (r, 0, 0))
    return pl.pallas_call(
        functools.partial(edges_kernel, scale),
        grid=(groups,),
        in_specs=[
            whole(nodes, width),
            whole(nodes, width),
            by_rel(batch, width),
            by_rel(width, width),
            by_rel(1, msgs),
            by_rel(1, msgs),
        ],
        out_specs=[
            by_rel(msgs, width),
            by_rel(msgs, width),
            by_rel(msgs, 128),
            whole(batch, width),
        ],
        out_shape=[
            jax.ShapeDtypeStruct((groups, msgs, width), BF),
            jax.ShapeDtypeStruct((groups, msgs, width), BF),
            jax.ShapeDtypeStruct((groups, msgs, 128), jnp.int32),
            jax.ShapeDtypeStruct((batch, width), F32),
        ],
        compiler_params=params(),
        cost_estimate=cost(2 * groups * msgs * width * (nodes + 1.5 * width), 12e6),
        name="edges",
    )(features, history, mean, weights, src, dst)


def partial_kernel(first, theirs, added, batch, pos, dst, sent, local, *rest):
    out = rest[-1]
    second = pl.program_id(0)
    half = batch // 2
    core = 1 - pos[3] if theirs else pos[3]
    rows = lax.broadcasted_iota(jnp.int32, (half, dst.shape[1]), 0)
    hot = []
    for depth in range(DEPTH):
        base = owner_of(pos, core, first, second, depth) * batch + core * half
        hot.append((dst[...] - base == rows).astype(F32).astype(BF))
    total = dot(jnp.concatenate(hot, axis=0), sent[...])
    if added:
        total = total + rest[0][...].astype(F32)
    out[...] = total.astype(out.dtype)
    if first == 0:

        @pl.when(second == 0)
        def _():
            own = local[pl.ds(pl.multiple_of(core * half, half), half), :]
            out[:half, :] = (total[:half] + own).astype(out.dtype)


def partial_rows(pos, dst, sent, local, first, theirs, added, dtype):
    batch, width = local.shape
    count = sent.shape[0]
    rows = DEPTH * batch // 2
    whole = lambda *shape: pl.BlockSpec(shape, lambda s, pos: (0,) * len(shape))
    piece = pl.BlockSpec((rows, width), lambda s, pos: (s, 0))
    more = [] if added is None else [added]
    return pl.pallas_call(
        functools.partial(partial_kernel, first, theirs, added is not None, batch),
        grid_spec=pltpu.PrefetchScalarGridSpec(
            num_scalar_prefetch=1,
            grid=(SIDE,),
            in_specs=[whole(1, count), whole(count, width), whole(batch, width)] + [piece] * len(more),
            out_specs=piece,
        ),
        out_shape=jax.ShapeDtypeStruct((SIDE * rows, width), dtype),
        compiler_params=params(),
        cost_estimate=cost(2 * SIDE * rows * width * count, 8e6),
        name="partial_rows",
    )(pos, dst, sent, local, *more)


def pick_kernel(layout, chained, batch, pos, spread, *rest):
    out = rest[-1]
    half = batch // 2
    lanes = lax.broadcasted_iota(jnp.int32, (spread.shape[1], half), 1)
    total = rest[-2][0].astype(F32) if chained else None
    for ref, (theirs, blocks) in zip(rest, layout):
        core = 1 - pos[3] if theirs else pos[3]
        hot = []
        for first, second, depth in blocks:
            base = owner_of(pos, core, first, second, -depth) * batch + core * half
            hot.append((spread[0] == lanes + base).astype(F32).astype(BF))
        term = dot(jnp.concatenate(hot, axis=1) if len(hot) > 1 else hot[0], ref[...])
        total = term if total is None else total + term
    out[0] = total.astype(BF)


def pick(pos, spread, batch, pieces, layout, before):
    groups, msgs, _ = spread.shape
    width = pieces[0].shape[1]
    by_rel = lambda *shape: pl.BlockSpec((1,) + shape, lambda r, pos: (r, 0, 0))
    more = [] if before is None else [before]
    rows = sum(piece.shape[0] for piece in pieces)
    return pl.pallas_call(
        functools.partial(pick_kernel, layout, before is not None, batch),
        grid_spec=pltpu.PrefetchScalarGridSpec(
            num_scalar_prefetch=1,
            grid=(groups,),
            in_specs=[by_rel(msgs, 128)]
            + [pl.BlockSpec(piece.shape, lambda r, pos: (0, 0)) for piece in pieces]
            + [by_rel(msgs, width)] * len(more),
            out_specs=by_rel(msgs, width),
        ),
        out_shape=jax.ShapeDtypeStruct((groups, msgs, width), BF),
        compiler_params=params(),
        cost_estimate=cost(2 * groups * msgs * width * rows, 6e6),
        name="pick_rows",
    )(pos, spread, *pieces, *more)


def back_kernel(scale, picked, weight, src, out):
    step = pl.program_id(0)
    grads = (scale * dot(picked[0], weight[0], ((1,), (1,)))).astype(BF)
    rows = lax.broadcasted_iota(jnp.int32, (out.shape[0], src.shape[2]), 0)
    term = dot((src[0] == rows).astype(F32).astype(BF), grads)

    @pl.when(step == 0)
    def _():
        out[...] = term

    @pl.when(step > 0)
    def _():
        out[...] += term


def back(picked, weights, src, nodes, scale):
    groups, msgs, width = picked.shape
    by_rel = lambda *shape: pl.BlockSpec((1,) + shape, lambda r: (r, 0, 0))
    return pl.pallas_call(
        functools.partial(back_kernel, scale),
        grid=(groups,),
        in_specs=[by_rel(msgs, width), by_rel(width, width), by_rel(1, msgs)],
        out_specs=pl.BlockSpec((nodes, width), lambda r: (0, 0)),
        out_shape=jax.ShapeDtypeStruct((nodes, width), F32),
        compiler_params=params(),
        cost_estimate=cost(2 * groups * msgs * width * (nodes + width), 8e6),
        name="feature_terms",
    )(picked, weights, src)


def weight_kernel(scale, norm, pos, mean, moved, cot, picked, away, kept):
    width = mean.shape[2]
    half = width // 2
    place = jnp.where(pos[3] == 0, pos[1], pos[2])
    for out, index in ((away, 1 - place), (kept, place)):
        columns = pl.ds(pl.multiple_of(index * half, 128), half)
        near = dot(mean[0, :, columns], cot[...], ((0,), (0,)))
        far = dot(moved[0, :, columns], picked[0], ((0,), (0,)))
        out[...] = (norm * (near + scale * far)).astype(out.dtype)


def weight_terms(pos, mean, moved, cot, picked, rel, scale, norm):
    _, batch, width = mean.shape
    msgs = moved.shape[1]
    by_rel = lambda *shape: pl.BlockSpec((1,) + shape, lambda s, pos: (rel, 0, 0))
    whole = lambda *shape: pl.BlockSpec(shape, lambda s, pos: (0,) * len(shape))
    return pl.pallas_call(
        functools.partial(weight_kernel, scale, norm),
        grid_spec=pltpu.PrefetchScalarGridSpec(
            num_scalar_prefetch=1,
            grid=(1,),
            in_specs=[by_rel(batch, width), by_rel(msgs, width), whole(batch, width), by_rel(msgs, width)],
            out_specs=[whole(width // 2, width), whole(width // 2, width)],
        ),
        out_shape=[
            jax.ShapeDtypeStruct((width // 2, width), BF),
            jax.ShapeDtypeStruct((width // 2, width), F32),
        ],
        compiler_params=params(),
        cost_estimate=cost(2 * width * width * (batch + msgs), 5e6),
        name="weight_terms",
    )(pos, mean, moved, cot, picked)


def assemble_kernel(pos, *refs):
    out = refs[-1]
    z, y, x, core = pos[0], pos[1], pos[2], pos[3]
    first = jnp.where(core == 0, y, x)
    second = jnp.where(core == 0, x, y)
    block = refs[0].shape[0]

    def put(row, value):
        out[0, pl.ds(pl.multiple_of(row, 16), value.shape[0]), :] = value.astype(F32)

    for ref, (flip_a, flip_b) in zip(refs[:4], ((0, 0), (0, 1), (1, 0), (1, 1))):
        a = first if flip_a == 0 else 1 - first
        b = second if flip_b == 0 else 1 - second
        for k in range(DEPTH):
            row = ((a * 2 + b) * DEPTH + lax.rem(z - k + DEPTH, DEPTH)) * (block // DEPTH)
            put(row, ref[k * (block // DEPTH) : (k + 1) * (block // DEPTH), :])


def assemble(pos, pieces, rel, groups, before):
    block, width = pieces[0].shape
    whole = lambda *shape: pl.BlockSpec(shape, lambda s, pos: (0,) * len(shape))
    more = [] if before is None else [before]
    return pl.pallas_call(
        assemble_kernel,
        grid_spec=pltpu.PrefetchScalarGridSpec(
            num_scalar_prefetch=1,
            grid=(1,),
            in_specs=[whole(block, width)] * 4 + [pl.BlockSpec(memory_space=pl.ANY)] * len(more),
            out_specs=pl.BlockSpec((1, width, width), lambda s, pos: (rel, 0, 0)),
        ),
        out_shape=jax.ShapeDtypeStruct((groups, width, width), F32),
        input_output_aliases={5: 0} if more else {},
        compiler_params=params(),
        cost_estimate=cost(0, 4e6),
        name="assemble",
    )(pos, *pieces, *more)


def body(
    features, history, history_mean, weights, source_rows, target_owner, target_rows, cotangent
):
    groups, width, _ = weights.shape
    batch = history_mean.shape[1]
    nodes = features.shape[0]
    msgs = source_rows.shape[1]
    owners = lax.axis_size("node")
    scale = 1.0 / (msgs // batch)
    dst = target_owner[:, :, 0] * batch + target_rows
    if owners != NODES_HERE:
        return anywhere(
            features, history, history_mean, weights, source_rows, dst, cotangent, scale
        )
    norm = (batch * owners) ** -0.5
    node = lax.axis_index("node")
    core = lax.axis_index("rel")
    z = node // 4
    pos = jnp.stack([z, node // 2 % 2, node % 2, core]).astype(jnp.int32)
    half = batch // 2
    src3, dst3 = source_rows[:, None, :], dst[:, None, :]

    mine = lax.dynamic_slice_in_dim(cotangent, core * half, half)
    other = lax.dynamic_slice_in_dim(cotangent, (1 - core) * half, half)
    deep = jnp.concatenate([hop(mine, ALONG[k]) for k in range(1, DEPTH)])
    near_b = hop(mine, SECOND)
    near_a = hop(mine, FIRST)
    near_ab = hop(near_b, FIRST)
    near = jnp.concatenate([near_a, near_b, near_ab])
    deep_b = hop(deep, SECOND)
    deep_a = hop(deep, FIRST)
    deep_ab = hop(deep_b, FIRST)

    moved, sent, spread, local = edges(
        features, history, history_mean, weights, src3, dst3, scale
    )
    flat = sent.reshape(groups * msgs, width)
    flat_dst = dst.reshape(1, groups * msgs)
    part = functools.partial(partial_rows, pos, flat_dst, flat, local)
    from_1 = hop(part(1, True, None, BF), CORES)
    from_0 = hop(part(0, True, None, BF), CORES)
    away = part(1, False, from_1, BF)
    kept = part(0, False, from_0, F32)

    swap = lambda array: hop(array, CORES)
    depths = tuple(range(1, DEPTH))
    near_blocks = ((1, 0, 0), (0, 1, 0), (1, 1, 0))
    at = lambda a, b: tuple((a, b, k) for k in depths)
    choose = functools.partial(pick, pos, spread, batch)
    picked = choose(
        [mine, other, near, swap(near)],
        ((False, ((0, 0, 0),)), (True, ((0, 0, 0),)), (False, near_blocks), (True, near_blocks)),
        None,
    )
    picked = choose([deep, swap(deep)], ((False, at(0, 0)), (True, at(0, 0))), picked)
    picked = choose(
        [deep_a, deep_b, swap(deep_a), swap(deep_b)],
        ((False, at(1, 0)), (False, at(0, 1)), (True, at(1, 0)), (True, at(0, 1))),
        picked,
    )
    picked = choose([deep_ab, swap(deep_ab)], ((False, at(1, 1)), (True, at(1, 1))), picked)

    kept = kept + hop(away, FIRST).astype(F32)
    rows = DEPTH * half
    kept = kept[:rows] + hop(kept[rows:].astype(BF), SECOND).astype(F32)
    total = kept[:half]
    for k in range(1, DEPTH):
        total = total + hop(kept[k * half : (k + 1) * half].astype(BF), ALONG[k]).astype(F32)
    total = total.astype(BF)
    opposite = hop(total, CORES)
    layer_out = jnp.where(
        core == 0, jnp.concatenate([total, opposite]), jnp.concatenate([opposite, total])
    )

    grads = None
    quarter = width // 4
    block = quarter // DEPTH
    place_b = jnp.where(core == 0, node % 2, node // 2 % 2)
    for rel in range(groups):
        away, kept = weight_terms(
            pos, history_mean, moved, cotangent, picked, rel, scale, norm
        )
        kept = kept + hop(away, FIRST).astype(F32)
        away = lax.dynamic_slice_in_dim(kept, (1 - place_b) * quarter, quarter).astype(BF)
        kept = lax.dynamic_slice_in_dim(kept, place_b * quarter, quarter)
        kept = kept + hop(away, SECOND).astype(F32)
        take = lambda k: lax.dynamic_slice_in_dim(kept, (z + k) % DEPTH * block, block)
        total = take(0)
        for k in range(1, DEPTH):
            total = total + hop(take(k).astype(BF), ALONG[k]).astype(F32)
        total = total.astype(BF)
        line = jnp.concatenate([total] + [hop(total, ALONG[k]) for k in range(1, DEPTH)])
        line_b = hop(line, SECOND)
        line_a = hop(line, FIRST)
        line_ab = hop(line_b, FIRST)
        grads = assemble(pos, [line, line_b, line_a, line_ab], rel, groups, grads)

    terms = back(picked, weights, src3, nodes, scale)
    feature_grads = (terms + hop(terms, CORES)).astype(BF)
    return layer_out, grads, feature_grads


def anywhere(features, history, history_mean, weights, source_rows, dst, cotangent, scale):
    groups, width, _ = weights.shape
    batch, nodes = cotangent.shape[0], features.shape[0]
    total_batch = batch * lax.axis_size("node")
    deltas = (features.astype(F32) - history.astype(F32)).astype(BF)
    every = lax.all_gather(cotangent, "node", tiled=True)
    out = jnp.zeros((total_batch, width), F32)
    local = jnp.zeros((batch, width), F32)
    terms = jnp.zeros((nodes, width), F32)
    grads = []
    for rel in range(groups):
        rows = jnp.take(deltas, source_rows[rel], axis=0)
        picked = jnp.take(every, dst[rel], axis=0)
        out = out.at[dst[rel]].add(scale * dot(rows, weights[rel]))
        local = local + dot(history_mean[rel], weights[rel])
        edge = (scale * dot(picked, weights[rel], ((1,), (1,)))).astype(BF)
        terms = terms.at[source_rows[rel]].add(edge.astype(F32))
        grads.append(
            dot(history_mean[rel], cotangent, ((0,), (0,)))
            + scale * dot(rows, picked, ((0,), (0,)))
        )
    layer_out = lax.psum(lax.psum_scatter(out, "node", tiled=True) + local, "rel").astype(BF)
    weight_grads = lax.psum(jnp.stack(grads) * total_batch**-0.5, "node")
    return layer_out, weight_grads, lax.psum(terms, "rel").astype(BF)


def solution(mesh):
    in_specs = (
        P("node", None),
        P("node", None),
        P("rel", "node", None),
        P("rel", None, None),
        P("rel", "node"),
        P("rel", "node", None),
        P("rel", "node"),
        P("node", None),
    )
    out_specs = (P("node", None), P("rel", None, None), P("node", None))
    return jax.shard_map(body, mesh=mesh, in_specs=in_specs, out_specs=out_specs, check_vma=False)
```

```python
import functools

import jax
import jax.numpy as jnp
from jax import lax
from jax.experimental import pallas as pl
from jax.experimental.pallas import tpu as pltpu
from jax.sharding import PartitionSpec as P

BF = jnp.bfloat16
F32 = jnp.float32
AXES = ("node", "rel")
DEPTH, SIDE = 4, 2
CHUNKS = 2
ORDER = (
    (0, 0),
    ("back", 0),
    (1, 0),
    (0, 1),
    ("rows", -1),
    (0, 2),
    (1, 1),
    (0, 3),
    (1, 2),
    (0, 4),
    (1, 3),
    ("rows", 0),
    (0, 5),
    (1, 4),
    ("rows", 1),
    (0, 6),
    (1, 5),
    ("rows", 2),
    (1, 6),
    (0, 7),
    ("rows", 3),
    ("back", 1),
    ("rows", 4),
    (1, 7),
)
NODES_HERE = DEPTH * SIDE * SIDE


def dot(a, b, dims=((1,), (0,))):
    return lax.dot_general(a, b, (dims, ((), ())), preferred_element_type=F32)


def call(name, kernel, pos, ins, outs, grid=(1,), after=(), alias=None, limit=24):
    def spec(block, index):
        if block is None:
            return pl.BlockSpec(memory_space=pl.ANY)
        if index is None:
            return pl.BlockSpec(block, lambda *_: (0,) * len(block))
        return pl.BlockSpec(block, index)

    many = len(ins)

    def run(pos_ref, *refs):
        kernel(pos_ref, *refs[:many], *refs[many + len(after) :])

    return pl.pallas_call(
        run,
        grid_spec=pltpu.PrefetchScalarGridSpec(
            num_scalar_prefetch=1,
            grid=grid,
            in_specs=[spec(block, index) for _, block, index in ins]
            + [pl.BlockSpec(memory_space=pl.ANY)] * len(after),
            out_specs=[spec(block, index) for _, _, block, index in outs],
        ),
        out_shape=[jax.ShapeDtypeStruct(shape, dtype) for shape, dtype, _, _ in outs],
        input_output_aliases=alias or {},
        compiler_params=pltpu.CompilerParams(
            dimension_semantics=("arbitrary",) * len(grid), vmem_limit_bytes=limit * 1024 * 1024
        ),
        cost_estimate=pl.CostEstimate(flops=1000, bytes_accessed=1000, transcendentals=0),
        name=name,
    )(pos, *[array for array, _, _ in ins], *after)


def full(array):
    return (array, array.shape, None)


def out(shape, dtype):
    return (shape, dtype, shape, None)


def gate(pos, arrays, after):
    return call(
        "gate",
        lambda *_: None,
        pos,
        [(array, None, None) for array in arrays],
        [(array.shape, array.dtype, None, None) for array in arrays],
        after=after,
        alias={i + 1: i for i in range(len(arrays))},
        limit=24,
    )


def pairs(move):
    listed = []
    for node in range(NODES_HERE):
        for core in range(2):
            z, y, x = node // 4, node // 2 % 2, node % 2
            tz, ty, tx, tc = move(z, y, x, core)
            listed.append((node * 2 + core, (tz * 4 + ty * 2 + tx) * 2 + tc))
    return listed


FIRST = pairs(lambda z, y, x, c: (z, y ^ (1 - c), x ^ c, c))
SECOND = pairs(lambda z, y, x, c: (z, y ^ c, x ^ (1 - c), c))
ALONG = [pairs(lambda z, y, x, c, k=k: (z ^ k, y, x, c)) for k in range(DEPTH)]
LINE = (0, 2, 1, 3)
CORES = pairs(lambda z, y, x, c: (z, y, x, 1 - c))


def hop(array, table):
    return lax.ppermute(array, AXES, table)


def owner_of(pos_ref, core, first, second, depth):
    y = pos_ref[1] ^ jnp.where(core == 0, first, second)
    x = pos_ref[2] ^ jnp.where(core == 0, second, first)
    return (pos_ref[0] ^ depth) * 4 + y * 2 + x


def by_rel(array):
    return (array, (1,) + array.shape[1:], lambda r, pos: (r, 0, 0))


def out_by_rel(groups, rows, width, dtype):
    return ((groups, rows, width), dtype, (1, rows, width), lambda r, pos: (r, 0, 0))


def split_kernel(pos, cot, mine):
    half = mine.shape[0]
    mine[...] = cot[pl.ds(pl.multiple_of(pos[3] * half, half), half), :]


def split(pos, cot):
    shape = (cot.shape[0] // 2, cot.shape[1])
    return call("split", split_kernel, pos, [full(cot)], [out(shape, BF)], limit=24)[0]


def join_kernel(pos, *refs):
    start = 0
    for ref in refs[:-1]:
        refs[-1][start : start + ref.shape[0], :] = ref[...]
        start += ref.shape[0]


def join(pos, pieces, after=()):
    shape = (sum(piece.shape[0] for piece in pieces), pieces[0].shape[1])
    return call(
        "join", join_kernel, pos, [full(p) for p in pieces], [out(shape, BF)], after=after, limit=8
    )[0]


def one_hot(values, places):
    return (values == places).astype(F32).astype(BF)


def partial_step(pos, core, first, second, batch, dst, sent, local):
    half = batch // 2
    rows = lax.broadcasted_iota(jnp.int32, (half, dst.shape[1]), 0)
    hot = []
    for depth in LINE:
        base = owner_of(pos, core, first, second, depth) * batch + core * half
        hot.append(one_hot(dst[...] - base, rows))
    total = dot(jnp.concatenate(hot, axis=0), sent[...])
    own = local[pl.ds(pl.multiple_of(core * half, half), half), :]
    here = (first + second == 0).astype(F32)
    return jnp.concatenate([total[:half] + here * own, total[half:]], axis=0)


def edges_kernel(scale, groups, batch, pos, feat, hist, mean, weight, src, dst, moved, sent, local, theirs):
    step = pl.program_id(0)
    nodes, msgs = feat.shape[0], src.shape[2]

    @pl.when(step < groups)
    def _():
        deltas = (feat[...].astype(F32) - hist[...].astype(F32)).astype(BF)
        column = jnp.transpose(jnp.broadcast_to(src[0], (128, msgs)))
        lanes = lax.broadcasted_iota(jnp.int32, (msgs, 128), 1)
        hot = jnp.concatenate([one_hot(column, lanes + n) for n in range(0, nodes, 128)], axis=1)
        rows = dot(hot, deltas).astype(BF)
        moved[0] = rows
        span = pl.ds(pl.multiple_of(step * msgs, msgs), msgs)
        sent[span, :] = (scale * dot(rows, weight[0])).astype(BF)
        own = dot(mean[0], weight[0])
        local[...] = jnp.where(step == 0, own, local[...] + own)

    @pl.when(step >= groups)
    def _():
        part = step - groups
        total = partial_step(pos, 1 - pos[3], 1 - part // 2, part % 2, batch, dst, sent, local)
        theirs[...] = total.astype(BF)


def edges(pos, features, history, mean, weights, src, dst, scale, after):
    groups, width, _ = weights.shape
    batch, msgs = mean.shape[1], src.shape[2]
    rows = DEPTH * batch // 2
    rel = lambda *shape: ((1,) + shape, lambda s, pos: (jnp.minimum(s, groups - 1), 0, 0))
    return call(
        "edges",
        functools.partial(edges_kernel, scale, groups, batch),
        pos,
        [
            full(features),
            full(history),
            (mean,) + rel(batch, width),
            (weights,) + rel(width, width),
            (src,) + rel(1, msgs),
            full(dst),
        ],
        [
            ((groups, msgs, width), BF) + rel(msgs, width),
            out((groups * msgs, width), BF),
            out((batch, width), F32),
            ((4 * rows, width), BF, (rows, width), lambda s, pos: (jnp.maximum(s - groups, 0), 0)),
        ],
        grid=(groups + 4,),
        after=after,
    )


def pick_step(pos, core, batch, column, pieces, layout):
    half = batch // 2
    lanes = lax.broadcasted_iota(jnp.int32, (column.shape[0], half), 1)
    total = None
    for ref, blocks in zip(pieces, layout):
        hot = []
        for first, second, depth in blocks:
            base = owner_of(pos, core, first, second, depth) * batch + core * half
            hot.append(one_hot(column, lanes + base))
        term = dot(jnp.concatenate(hot, axis=1) if len(hot) > 1 else hot[0], ref[...])
        total = term if total is None else total + term
    return total


def early_kernel(layout, groups, batch, pos, dst, flat, sent, local, *refs):
    pieces, (spread, theirs, own, part) = refs[: len(layout)], refs[len(layout) :]
    step = pl.program_id(0)
    msgs = dst.shape[2]

    @pl.when(step < 2 * groups)
    def _():
        column = jnp.transpose(jnp.broadcast_to(dst[0], (128, msgs)))
        spread[0] = column
        rows = pick_step(pos, pos[3], batch, column, pieces, layout).astype(BF)

        @pl.when(step < groups)
        def _():
            theirs[0] = rows

        @pl.when(step >= groups)
        def _():
            own[0] = rows

    @pl.when(step >= 2 * groups)
    def _():
        at = step - 2 * groups
        part[...] = partial_step(pos, pos[3], 1 - at // 2, at % 2, batch, flat, sent, local)


def halves(groups, msgs, width):
    return (
        ((1, msgs, width), lambda s, pos: (jnp.clip(s, 0, groups - 1), 0, 0)),
        ((1, msgs, width), lambda s, pos: (jnp.clip(s - groups, 0, groups - 1), 0, 0)),
    )


def pick_early(pos, dst, flat, sent, local, pieces, layout, after):
    count, _, msgs = dst.shape
    groups = count // 2
    batch, width = local.shape
    rows = DEPTH * batch // 2
    every = lambda *shape: ((1,) + shape, lambda s, pos: (jnp.minimum(s, count - 1), 0, 0))
    theirs, own = halves(groups, msgs, width)
    return call(
        "pick_early",
        functools.partial(early_kernel, layout, groups, batch),
        pos,
        [(dst,) + every(1, msgs), full(flat), full(sent), full(local)] + [full(p) for p in pieces],
        [
            ((count, msgs, 128), jnp.int32) + every(msgs, 128),
            ((groups, msgs, width), BF) + theirs,
            ((groups, msgs, width), BF) + own,
            ((4 * rows, width), F32, (rows, width), lambda s, pos: (jnp.maximum(s - count, 0), 0)),
        ],
        grid=(count + 4,),
        after=after,
    )


def middle_kernel(layout, groups, batch, pos, spread, theirs, own, *refs):
    pieces, (theirs_out, own_out) = refs[: len(layout)], refs[len(layout) :]
    step = pl.program_id(0)
    rows = pick_step(pos, pos[3], batch, spread[0], pieces, layout)

    @pl.when(step < groups)
    def _():
        theirs_out[0] = (rows + theirs[0].astype(F32)).astype(BF)

    @pl.when(step >= groups)
    def _():
        own_out[0] = (rows + own[0].astype(F32)).astype(BF)


def pick_middle(pos, spread, theirs, own, batch, pieces, layout, after):
    groups, msgs, width = own.shape
    a, b = halves(groups, msgs, width)
    return call(
        "pick_middle",
        functools.partial(middle_kernel, layout, groups, batch),
        pos,
        [by_rel(spread), (theirs,) + a, (own,) + b] + [full(p) for p in pieces],
        [(own.shape, BF) + a, (own.shape, BF) + b],
        grid=(2 * groups,),
        after=after,
    )


def last_kernel(blocks, batch, pos, spread, own, piece, result):
    rows = pick_step(pos, pos[3], batch, spread[0], [piece], [blocks])
    result[0] = (rows + own[0].astype(F32)).astype(BF)


def pick_last(pos, spread, own, batch, piece, blocks, after):
    groups, msgs, _ = own.shape
    return call(
        "pick_last",
        functools.partial(last_kernel, blocks, batch),
        pos,
        [(spread, (1, msgs, 128), lambda s, pos: (groups + s, 0, 0)), by_rel(own), full(piece)],
        [(own.shape, BF) + by_rel(own)[1:]],
        grid=(groups,),
        after=after,
    )[0]


def back_kernel(scale, pos, picked, weight, src, result):
    step = pl.program_id(0)
    grads = (scale * dot(picked[0], weight[0], ((1,), (1,)))).astype(BF)
    rows = lax.broadcasted_iota(jnp.int32, (result.shape[0], src.shape[2]), 0)
    term = dot((src[0] == rows).astype(F32).astype(BF), grads)

    @pl.when(step == 0)
    def _():
        result[...] = term

    @pl.when(step > 0)
    def _():
        result[...] += term


def back(pos, picked, weights, src, nodes, scale, after):
    groups, _, width = picked.shape
    return call(
        "feature_terms",
        functools.partial(back_kernel, scale),
        pos,
        [by_rel(picked), by_rel(weights), by_rel(src)],
        [out((nodes, width), F32)],
        grid=(groups,),
        after=after,
    )[0]


def sum_kernel(pos, one, two, result):
    result[...] = (one[...].astype(F32) + two[...].astype(F32)).astype(result.dtype)


def rows_zero_kernel(pos, part, came, *away):
    total = (part[...] + came[...].astype(F32)).astype(BF)

    @pl.when(pl.program_id(0) == 0)
    def _():
        away[0][...] = total

    @pl.when(pl.program_id(0) == 1)
    def _():
        away[1][...] = total


def rows_zero(pos, part, came, after):
    rows = (part.shape[0] // 4, part.shape[1])
    block = (rows, lambda s, pos: (s, 0))
    return call(
        "rows_zero",
        rows_zero_kernel,
        pos,
        [(part,) + block, (came,) + block],
        [out(rows, BF), out(rows, BF)],
        grid=(2,),
        after=after,
    )


def rows_first_kernel(pos, part, passed, came, come, stay, away):
    rows = stay.shape[0]
    for ref, one, span in ((stay, came, slice(0, rows)), (away, come, slice(rows, 2 * rows))):
        total = part[span, :] + passed[span, :].astype(F32) + one[...].astype(F32)
        ref[...] = total.astype(ref.dtype)


def rows_first(pos, part, passed, came, after):
    rows = part.shape[0] // 2
    last = lambda array: (array, (rows, array.shape[1]), lambda s, pos: (1, 0))
    shape = (rows // 2, part.shape[1])
    return call(
        "rows_first",
        rows_first_kernel,
        pos,
        [last(part), last(passed), full(came[0]), full(came[1])],
        [out(shape, F32), out(shape, BF)],
        after=after,
    )


def rows_fold_kernel(pos, kept, came, stay, away):
    rows = stay.shape[0]
    for ref, span in ((stay, slice(0, rows)), (away, slice(rows, 2 * rows))):
        ref[...] = (kept[span, :] + came[span, :].astype(F32)).astype(ref.dtype)


def rows_fold(pos, kept, came, after):
    shape = (kept.shape[0] // 2, kept.shape[1])
    return call(
        "rows_fold",
        rows_fold_kernel,
        pos,
        [full(kept), full(came)],
        [out(shape, F32), out(shape, BF)],
        after=after,
    )


def line_sum_kernel(pos, kept, *refs):
    total = kept[...]
    for ref in refs[:-1]:
        total = total + ref[...].astype(F32)
    refs[-1][...] = total.astype(BF)


def line_sum(pos, kept, came, after):
    return call(
        "line_sum",
        line_sum_kernel,
        pos,
        [full(kept)] + [full(piece) for piece in came],
        [out(kept.shape, BF)],
        after=after,
        limit=24,
    )[0]


def finish_kernel(pos, total, opposite, result):
    half = total.shape[0]
    result[pl.ds(pl.multiple_of(pos[3] * half, half), half), :] = total[...]
    result[pl.ds(pl.multiple_of((1 - pos[3]) * half, half), half), :] = opposite[...]


def finish(pos, total, opposite, after):
    shape = (total.shape[0] * 2, total.shape[1])
    return call(
        "finish", finish_kernel, pos, [full(total), full(opposite)], [out(shape, BF)], after=after, limit=8
    )[0]


def weight_kernel(scale, norm, blocks, batch, pos, spread, own, came, far, mean, moved, cot, *refs):
    picked, away, kept = refs[-3:]
    total = pick_step(pos, 1 - pos[3], batch, spread[0], [far], [blocks])
    total = total + own[0].astype(F32) + came[0].astype(F32)
    rows = total.astype(BF)
    picked[0] = rows
    half = mean.shape[2] // 2
    place = jnp.where(pos[3] == 0, pos[1], pos[2])
    for ref, index in ((away, 1 - place), (kept, place)):
        columns = pl.ds(pl.multiple_of(index * half, 128), half)
        one = dot(mean[0, :, columns], cot[...], ((0,), (0,)))
        two = dot(moved[0, :, columns], rows, ((0,), (0,)))
        ref[0] = (norm * (one + scale * two)).astype(ref.dtype)


def weight_terms(pos, spread, own, came, far, blocks, mean, moved, cot, chunk, before, scale, norm, after):
    groups, msgs, width = moved.shape
    span = width // CHUNKS
    shape = (groups, width // 2, span)
    columns = lambda array: (array, (1, array.shape[1], span), lambda s, pos: (s, 0, chunk))
    flat = lambda array: (array, (array.shape[0], span), lambda s, pos: (0, chunk))
    block = ((1,) + shape[1:], lambda s, pos: (s, 0, 0))
    more = [] if before is None else [(before, None, None)]
    return call(
        "weight_terms",
        functools.partial(weight_kernel, scale, norm, blocks, cot.shape[0]),
        pos,
        [
            (spread, (1, msgs, 128), lambda s, pos: (groups + s, 0, 0)),
            columns(own),
            columns(came),
            flat(far),
            by_rel(mean),
            by_rel(moved),
            flat(cot),
        ]
        + more,
        [(own.shape, BF) + columns(own)[1:], (shape, BF) + block, (shape, F32) + block],
        grid=(groups,),
        after=after,
        alias={8: 0} if more else None,
    )


PLACES = (
    lambda pos: jnp.where(pos[3] == 0, pos[2], pos[1]),
    lambda pos: pos[0] % 2,
    lambda pos: pos[0] // 2,
)


def weight_fold_kernel(place, pos, kept, came, stay, away):
    rows = stay.shape[1]
    for ref, index in ((stay, place(pos)), (away, 1 - place(pos))):
        span = pl.ds(pl.multiple_of(index * rows, 16), rows)
        ref[...] = (kept[:, span, :] + came[:, span, :].astype(F32)).astype(ref.dtype)


def weight_fold(pos, kept, came, place, after):
    shape = (kept.shape[0], kept.shape[1] // 2, kept.shape[2])
    return call(
        "weight_fold",
        functools.partial(weight_fold_kernel, place),
        pos,
        [full(kept), full(came)],
        [out(shape, F32), out(shape, BF)],
        after=after,
    )


def assemble_kernel(pos, *refs):
    result = refs[-1]
    z, y, x, core = pos[0], pos[1], pos[2], pos[3]
    first = jnp.where(core == 0, y, x)
    second = jnp.where(core == 0, x, y)
    count = pl.num_programs(0)
    rows = result.shape[1] // NODES_HERE
    for flip_a, ref in enumerate(refs[:2]):
        for index in range(2 * DEPTH):
            flip_b, k = index // DEPTH, LINE[index % DEPTH]
            block = ((first ^ flip_a) * 2 + (second ^ flip_b)) * DEPTH + z % 2 * 2 + z // 2
            place = block ^ (k % 2 * 2 + k // 2)
            start = (index * count + pl.program_id(0)) * rows
            result[0, pl.ds(pl.multiple_of(place * rows, 16), rows), :] = ref[
                pl.ds(pl.multiple_of(start, 16), rows), :
            ].astype(F32)


def assemble(pos, pieces, chunk, groups, width, before, after):
    span = pieces[0].shape[1]
    more = [] if before is None else [(before, None, None)]
    return call(
        "assemble",
        assemble_kernel,
        pos,
        [full(piece) for piece in pieces] + more,
        [((groups, width, width), F32, (1, width, span), lambda s, pos: (s, 0, chunk))],
        grid=(groups,),
        after=[] if after[0] is before else after,
        alias={3: 0} if more else None,
    )[0]


def body(
    features, history, history_mean, weights, source_rows, target_owner, target_rows, cotangent
):
    groups, width, _ = weights.shape
    batch = history_mean.shape[1]
    nodes = features.shape[0]
    msgs = source_rows.shape[1]
    owners = lax.axis_size("node")
    scale = 1.0 / (msgs // batch)
    dst = target_owner[:, :, 0] * batch + target_rows
    if owners != NODES_HERE:
        return anywhere(
            features, history, history_mean, weights, source_rows, dst, cotangent, scale
        )
    norm = (batch * owners) ** -0.5
    node = lax.axis_index("node")
    core = lax.axis_index("rel")
    z = node // 4
    pos = jnp.stack([z, node // 2 % 2, node % 2, core]).astype(jnp.int32)
    half = batch // 2
    src3 = source_rows[:, None, :]
    flat = dst.reshape(1, groups * msgs)
    swap = lambda array: hop(array, CORES)
    at = lambda a, b: tuple((a, b, k) for k in range(DEPTH))

    both = jnp.concatenate([swap(dst), dst])[:, None, :]
    mine = split(pos, cotangent)
    deep = [mine] + [hop(mine, ALONG[k]) for k in range(1, DEPTH)]
    moved, sent, local, theirs = edges(
        pos, features, history, history_mean, weights, src3, flat, scale, [mine, both]
    )
    deep = join(pos, deep, [theirs])
    (theirs,) = gate(pos, [theirs], [deep])

    deep_b, deep_a, came = hop(deep, SECOND), hop(deep, FIRST), swap(theirs)
    spread, pick_o, pick_m, part = pick_early(
        pos, both, flat, sent, local, [deep], (at(0, 0),), [deep]
    )
    deep_b, deep_a, came = gate(pos, [deep_b, deep_a, came], [part])

    deep_ab = hop(deep_b, FIRST)
    pick_o, pick_m = pick_middle(
        pos, spread, pick_o, pick_m, batch, [deep_a, deep_b], (at(1, 0), at(0, 1)), [deep_b]
    )
    deep_ab, pick_o = gate(pos, [deep_ab, pick_o], [pick_m])
    deep_abo = swap(deep_ab)
    pick_c = swap(pick_o)
    pick_m = pick_last(pos, spread, pick_m, batch, deep_ab, at(1, 1), [deep_ab])

    chunks = [{"index": index} for index in range(CHUNKS)]
    last, picked = pick_m, None
    for chunk in chunks:
        picked, chunk["away"], chunk["kept"] = weight_terms(
            pos,
            spread,
            pick_m,
            pick_c,
            deep_abo,
            at(1, 1),
            history_mean,
            moved,
            cotangent,
            chunk["index"],
            picked,
            scale,
            norm,
            [last],
        )
        last = chunk["away"]
        chunk["came"] = hop(chunk["away"], FIRST)
    state = {"grads": None}
    FOLDS = (SECOND, ALONG[1], ALONG[2])

    def weight_step(chunk, step, last):
        if step < 3:
            chunk["kept"], away = weight_fold(
                pos, chunk["kept"], chunk["came"], PLACES[step], [last]
            )
            chunk["came"] = hop(away, FOLDS[step])
            return away
        if step == 3:
            total = line_sum(pos, chunk["kept"], [chunk["came"]], [last])
            total = total.reshape(-1, total.shape[2])
            chunk["line"] = [total, hop(total, ALONG[2])]
            return total
        if step < 7:
            line = join(pos, chunk["line"], [last])
            chunk["line"] = [line, hop(line, (ALONG[1], SECOND, FIRST)[step - 4])]
            return line
        state["grads"] = assemble(
            pos, chunk["line"], chunk["index"], groups, width, state["grads"], [last]
        )
        return state["grads"]

    def rows_step(step, last):
        if step == -1:
            aways = rows_zero(pos, part, came, [last])
            state["came"] = [hop(away, FIRST) for away in aways]
            return aways[0]
        if step == 0:
            state["kept"], away = rows_first(pos, part, came, state["came"], [last])
        elif step < 3:
            state["kept"], away = rows_fold(pos, state["kept"], state["came"], [last])
        if step < 3:
            state["came"] = hop(away, FOLDS[step])
            return away
        if step == 3:
            state["total"] = line_sum(pos, state["kept"], [state["came"]], [last])
            state["opposite"] = swap(state["total"])
            return state["total"]
        state["out"] = finish(pos, state["total"], state["opposite"], [last])
        return state["out"]

    def back_step(step, last):
        if step == 0:
            state["terms"] = back(pos, picked, weights, src3, nodes, scale, [last])
            state["terms_o"] = swap(state["terms"])
            return state["terms"]
        state["back"] = call(
            "sum",
            sum_kernel,
            pos,
            [full(state["terms"]), full(state["terms_o"])],
            [out((nodes, width), BF)],
            after=[last],
        )[0]
        return state["back"]

    for what, step in ORDER:
        if what == "rows":
            last = rows_step(step, last)
        elif what == "back":
            last = back_step(step, last)
        else:
            last = weight_step(chunks[what], step, last)
    return state["out"], state["grads"], state["back"]


def anywhere(features, history, history_mean, weights, source_rows, dst, cotangent, scale):
    groups, width, _ = weights.shape
    batch, nodes = cotangent.shape[0], features.shape[0]
    total_batch = batch * lax.axis_size("node")
    deltas = (features.astype(F32) - history.astype(F32)).astype(BF)
    every = lax.all_gather(cotangent, "node", tiled=True)
    out = jnp.zeros((total_batch, width), F32)
    local = jnp.zeros((batch, width), F32)
    terms = jnp.zeros((nodes, width), F32)
    grads = []
    for rel in range(groups):
        rows = jnp.take(deltas, source_rows[rel], axis=0)
        picked = jnp.take(every, dst[rel], axis=0)
        out = out.at[dst[rel]].add(scale * dot(rows, weights[rel]))
        local = local + dot(history_mean[rel], weights[rel])
        edge = (scale * dot(picked, weights[rel], ((1,), (1,)))).astype(BF)
        terms = terms.at[source_rows[rel]].add(edge.astype(F32))
        grads.append(
            dot(history_mean[rel], cotangent, ((0,), (0,)))
            + scale * dot(rows, picked, ((0,), (0,)))
        )
    layer_out = lax.psum(lax.psum_scatter(out, "node", tiled=True) + local, "rel").astype(BF)
    weight_grads = lax.psum(jnp.stack(grads) * total_batch**-0.5, "node")
    return layer_out, weight_grads, lax.psum(terms, "rel").astype(BF)


def solution(mesh):
    in_specs = (
        P("node", None),
        P("node", None),
        P("rel", "node", None),
        P("rel", None, None),
        P("rel", "node"),
        P("rel", "node", None),
        P("rel", "node"),
        P("node", None),
    )
    out_specs = (P("node", None), P("rel", None, None), P("node", None))
    return jax.shard_map(body, mesh=mesh, in_specs=in_specs, out_specs=out_specs, check_vma=False)
```

```python
import functools

import jax
import jax.numpy as jnp
from jax import lax
from jax.experimental import pallas as pl
from jax.experimental.pallas import tpu as pltpu
from jax.sharding import PartitionSpec as P

BF = jnp.bfloat16
F32 = jnp.float32
AXES = ("node", "rel")
DEPTH, SIDE = 4, 2
CHUNKS = 2
LIMIT = 24
ROUNDS = (
    (((0, 0),), (2,)),
    (((1, 0), (0, 1),), (3,)),
    (((0, 2), (1, 1), ("back", 0),), (1,)),
    (((0, 3), (1, 2), ("back", 2), ("back", 1),), (0,)),
    (((0, 4), (1, 3), ("back", 3), ("back", 4), ("rows", 0),), ()),
    (((0, 5), (1, 4), ("back", 5),), ()),
    (((0, 6), (1, 5), ("back", 6), ("rows", 1),), ()),
    (((1, 6), ("rows", 2),), ()),
    ((("rows", 3),), ()),
    ((("rows", 4),), ()),
)
NODES_HERE = DEPTH * SIDE * SIDE


def dot(a, b, dims=((1,), (0,))):
    return lax.dot_general(a, b, (dims, ((), ())), preferred_element_type=F32)


def call(name, kernel, pos, ins, outs, grid=(1,), after=(), alias=None, limit=24, scratch=()):
    def spec(block, index):
        if block is None:
            return pl.BlockSpec(memory_space=pl.ANY)
        if index is None:
            return pl.BlockSpec(block, lambda *_: (0,) * len(block))
        return pl.BlockSpec(block, index)

    many = len(ins)

    def run(pos_ref, *refs):
        kernel(pos_ref, *refs[:many], *refs[many + len(after) :])

    return pl.pallas_call(
        run,
        grid_spec=pltpu.PrefetchScalarGridSpec(
            num_scalar_prefetch=1,
            grid=grid,
            in_specs=[spec(block, index) for _, block, index in ins]
            + [pl.BlockSpec(memory_space=pl.ANY)] * len(after),
            out_specs=[spec(block, index) for _, _, block, index in outs],
            scratch_shapes=scratch,
        ),
        out_shape=[jax.ShapeDtypeStruct(shape, dtype) for shape, dtype, _, _ in outs],
        input_output_aliases=alias or {},
        compiler_params=pltpu.CompilerParams(
            dimension_semantics=("arbitrary",) * len(grid), vmem_limit_bytes=limit * 1024 * 1024
        ),
        cost_estimate=pl.CostEstimate(flops=1000, bytes_accessed=1000, transcendentals=0),
        name=name,
    )(pos, *[array for array, _, _ in ins], *after)


def full(array):
    return (array, array.shape, None)


def out(shape, dtype):
    return (shape, dtype, shape, None)


def together(pos, jobs, after):
    ins = [entry for _, job_ins, _, _ in jobs for entry in job_ins]
    outs = [entry for _, _, job_outs, _ in jobs for entry in job_outs]
    spans, alias, i, o = [], {}, 0, 0
    for _, job_ins, job_outs, job_alias in jobs:
        spans.append((i, i + len(job_ins), o, o + len(job_outs)))
        alias.update({1 + i + source: o + target for source, target in job_alias.items()})
        i, o = spans[-1][1], spans[-1][3]

    def kernel(pos_ref, *refs):
        for (work, _, _, _), (a, b, c, d) in zip(jobs, spans):
            work(pos_ref, *refs[a:b], *refs[len(ins) + c : len(ins) + d])

    results = call("step", kernel, pos, ins, outs, after=after, alias=alias, limit=LIMIT)
    return [results[c:d] for _, _, c, d in spans]


def gate_job(arrays):
    return (
        lambda *_: None,
        [(array, None, None) for array in arrays],
        [(array.shape, array.dtype, None, None) for array in arrays],
        {i: i for i in range(len(arrays))},
    )


def pairs(move):
    listed = []
    for node in range(NODES_HERE):
        for core in range(2):
            z, y, x = node // 4, node // 2 % 2, node % 2
            tz, ty, tx, tc = move(z, y, x, core)
            listed.append((node * 2 + core, (tz * 4 + ty * 2 + tx) * 2 + tc))
    return listed


FIRST = pairs(lambda z, y, x, c: (z, y ^ (1 - c), x ^ c, c))
SECOND = pairs(lambda z, y, x, c: (z, y ^ c, x ^ (1 - c), c))
ALONG = [pairs(lambda z, y, x, c, k=k: (z ^ k, y, x, c)) for k in range(DEPTH)]
LINE = (0, 2, 1, 3)
CORES = pairs(lambda z, y, x, c: (z, y, x, 1 - c))


def hop(array, table):
    return lax.ppermute(array, AXES, table)


def by_rel(array):
    return (array, (1,) + array.shape[1:], lambda r, pos: (r, 0, 0))


def out_by_rel(groups, rows, width, dtype):
    return ((groups, rows, width), dtype, (1, rows, width), lambda r, pos: (r, 0, 0))


def join_kernel(pos, *refs):
    start = 0
    for ref in refs[:-1]:
        refs[-1][start : start + ref.shape[0], :] = ref[...]
        start += ref.shape[0]


def copy_kernel(pos, source, target):
    target[...] = source[...]


def join_job(pieces):
    shape = (sum(piece.shape[0] for piece in pieces), pieces[0].shape[1])
    return (join_kernel, [full(piece) for piece in pieces], [out(shape, BF)], {})


def one_hot(values, places):
    return (values == places).astype(F32).astype(BF)


def partial_step(pos, core, first, second, batch, dst, sent, local):
    half = batch // 2
    rows = lax.broadcasted_iota(jnp.int32, (half, dst.shape[1]), 0)
    hot = []
    for depth in LINE:
        base = owner_of(pos, core, first, second, depth) * batch + core * half
        hot.append(one_hot(dst[...] - base, rows))
    total = dot(jnp.concatenate(hot, axis=0), sent[...])
    own = local[pl.ds(pl.multiple_of(core * half, half), half), :]
    here = (first + second == 0).astype(F32)
    return jnp.concatenate([total[:half] + here * own, total[half:]], axis=0)


def one_hot(values, places):
    return (values == places).astype(F32).astype(BF)


FIELDS = 4
EXTRA = 16
PART = 256


def fields(block, rel, count):
    places = lax.broadcasted_iota(jnp.int32, block.shape, 0)
    rows = [
        jnp.sum(jnp.where(places == rel * FIELDS + f, block, 0.0), axis=0, keepdims=True)
        for f in range(FIELDS)
    ]
    return [row[:, :count].astype(jnp.int32) for row in rows]


def prepare_kernel(pos, feat, hist, numbers, cot, mine, theirs, line):
    half = feat.shape[0] // 2
    for ref, core in ((mine, pos[3]), (theirs, 1 - pos[3])):
        span = pl.ds(pl.multiple_of(core * half, half), half)
        deltas = feat[span, :].astype(F32) - hist[span, :].astype(F32)
        ref[:half, :] = deltas.astype(BF)
        ref[half:, :] = jnp.zeros((EXTRA, ref.shape[1]), BF)
        ref[half:, : numbers.shape[1]] = numbers[...]
    half = line.shape[0]
    line[...] = cot[pl.ds(pl.multiple_of(pos[3] * half, half), half), :]


def prepare(pos, features, history, numbers, cot):
    nodes, width = features.shape
    shape = (nodes // 2 + EXTRA, width)
    return call(
        "prepare",
        prepare_kernel,
        pos,
        [full(features), full(history), full(numbers), full(cot)],
        [out(shape, BF), out(shape, BF), out((cot.shape[0] // 2, width), BF)],
        limit=24,
    )


def gather_step(pos, rel, msgs, mine, theirs):
    half = mine.shape[0] - EXTRA
    _, _, low, high = fields(mine[half:, :].astype(F32), rel, msgs)
    column = jnp.transpose(jnp.broadcast_to(low + PART * high, (128, msgs)))
    lanes = lax.broadcasted_iota(jnp.int32, (msgs, 128), 1)
    total = None
    for ref, core in ((mine, pos[3]), (theirs, 1 - pos[3])):
        hot = [one_hot(column, lanes + (core * half + n)) for n in range(0, half, 128)]
        term = dot(jnp.concatenate(hot, axis=1), ref[:half, :])
        total = term if total is None else total + term
    return total.astype(BF)


def gather_kernel(msgs, pos, *refs):
    result = refs[-1]
    for n in range(len(refs) // 2):
        result[0, n * msgs : (n + 1) * msgs, :] = gather_step(
            pos, pl.program_id(0), msgs, refs[2 * n], refs[2 * n + 1]
        )


def gather(pos, groups, msgs, pieces, places, after):
    rows, width = pieces[0].shape
    return call(
        "gather",
        functools.partial(gather_kernel, msgs),
        pos,
        [
            (piece, (rows, width), lambda r, pos, place=place: (place, 0))
            for piece, place in zip(pieces, places)
        ],
        [out_by_rel(groups, len(pieces) // 2 * msgs, width, BF)],
        grid=(groups,),
        after=after,
        limit=24,
    )[0]


def bases(pos, batch):
    half = batch // 2
    for core in (pos[3], 1 - pos[3]):
        for depth in LINE:
            owner = (pos[0] ^ depth) * SIDE * SIDE + pos[1] * SIDE + pos[2]
            yield owner * batch + core * half


def aggregate_part(scale, pos, batch, payloads, moved, side):
    rel = pl.program_id(0)
    half = batch // 2
    msgs = moved.shape[0] // len(payloads)
    dst = []
    for ref in payloads:
        owner, row, _, _ = fields(ref[ref.shape[0] - EXTRA :, :].astype(F32), rel, msgs)
        dst.append(owner * batch + row)
    dst = jnp.concatenate(dst, axis=1)
    rows = lax.broadcasted_iota(jnp.int32, (half, dst.shape[1]), 0)
    places = list(bases(pos, batch))[side * DEPTH : (side + 1) * DEPTH]
    hot = [one_hot(dst - base, rows) for base in places]
    return scale * dot(jnp.concatenate(hot, axis=0), moved)


def aggregate_near_kernel(scale, pos, own, near_a, near_b, one, two, mean, result):
    batch = mean.shape[1]
    half = batch // 2
    moved = jnp.concatenate([one[0], two[0]], axis=0)
    for side in range(2):
        total = aggregate_part(scale, pos, batch, [own, near_a, near_b], moved, side)
        core = pos[3] if side == 0 else 1 - pos[3]
        own_mean = mean[0, pl.ds(pl.multiple_of(core * half, half), half), :].astype(F32)
        at = side * DEPTH * half
        result[0, at : at + half, :] = total[:half] + own_mean
        result[0, at + half : at + DEPTH * half, :] = total[half:]


def aggregate_near(pos, mean, payloads, moved, scale, after):
    groups, batch, width = mean.shape
    return call(
        "aggregate_near",
        functools.partial(aggregate_near_kernel, scale),
        pos,
        [full(p) for p in payloads] + [by_rel(m) for m in moved] + [by_rel(mean)],
        [out_by_rel(groups, DEPTH * batch, width, F32)],
        grid=(groups,),
        after=after,
        limit=32,
    )[0]


def aggregate_kernel(scale, msgs, batch, pos, near_ab, far_ab, before, result):
    moved = gather_step(pos, pl.program_id(0), msgs, near_ab, far_ab)
    rows = DEPTH * batch // 2
    for side in range(2):
        span = slice(side * rows, (side + 1) * rows)
        total = aggregate_part(scale, pos, batch, [near_ab], moved, side)
        result[0, span, :] = (total + before[0, span, :]).astype(BF)


def aggregate(pos, msgs, batch, near_ab, far_ab, before, scale, after):
    groups, rows, width = before.shape
    return call(
        "aggregate",
        functools.partial(aggregate_kernel, scale, msgs, batch),
        pos,
        [full(near_ab), full(far_ab), by_rel(before)],
        [out_by_rel(groups, rows, width, BF)],
        grid=(groups,),
        after=after,
        limit=32,
    )[0]


def output_kernel(pos, sums, weight, result):
    total = dot(sums[0], weight[0])
    for rel in range(1, sums.shape[0]):
        total = total + dot(sums[rel], weight[rel])
    result[...] = total.astype(result.dtype)


def output_terms(pos, sums, weights, side, dtype, after):
    groups, rows, width = sums.shape
    return call(
        "output_terms",
        output_kernel,
        pos,
        [(sums, (groups, rows // 2, width), lambda s, pos: (0, side, 0)), full(weights)],
        [out((rows // 2, width), dtype)],
        after=after,
        limit=24,
    )[0]


def back_kernel(scale, batch, msgs, pos, payload, line, far, weight, kept, away, total):
    rel = pl.program_id(0)
    half = line.shape[0] // DEPTH
    owner, row, low, high = fields(
        payload[payload.shape[0] - EXTRA :, :].astype(F32), rel, msgs
    )
    column = jnp.transpose(jnp.broadcast_to(owner * batch + row, (128, msgs)))
    lanes = lax.broadcasted_iota(jnp.int32, (msgs, half), 1)
    hot = [one_hot(column, lanes + base) for base in bases(pos, batch)]
    picked = dot(jnp.concatenate(hot[:DEPTH], axis=1), line[...])
    picked = picked + dot(jnp.concatenate(hot[DEPTH:], axis=1), far[...])
    grads = (scale * dot(picked.astype(BF), weight[0], ((1,), (1,)))).astype(BF)
    rows = lax.broadcasted_iota(jnp.int32, (total.shape[0], msgs), 0)
    term = dot(one_hot(low + PART * high, rows), grads)

    @pl.when(rel == 0)
    def _():
        total[...] = term

    @pl.when(rel > 0)
    def _():
        total[...] += term

    @pl.when(rel == pl.num_programs(0) - 1)
    def _():
        size = kept.shape[0]
        kept[...] = total[pl.ds(pl.multiple_of(pos[3] * size, size), size), :]
        away[...] = total[pl.ds(pl.multiple_of((1 - pos[3]) * size, size), size), :].astype(BF)


def back_terms(pos, batch, msgs, payload, line, far, weights, scale, after):
    groups, width, _ = weights.shape
    half = payload.shape[0] - EXTRA
    return call(
        "feature_terms",
        functools.partial(back_kernel, scale, batch, msgs),
        pos,
        [full(payload), full(line), full(far), by_rel(weights)],
        [out((half, width), F32), out((half, width), BF)],
        grid=(groups,),
        after=after,
        scratch=[pltpu.VMEM((2 * half, width), F32)],
        limit=24,
    )


def sum_kernel(pos, *refs):
    total = refs[0][...].astype(F32)
    for ref in refs[1:-1]:
        total = total + ref[...].astype(F32)
    refs[-1][...] = total.astype(refs[-1].dtype)


def sum_rows_job(terms, dtype):
    shape = terms[0][0].shape
    ins = [(array, shape, lambda s, pos, place=place: (place, 0)) for array, place in terms]
    return (sum_kernel, ins, [out(shape, dtype)], {})


def sum_pair_kernel(pos, one, two, came, result):
    rows = one.shape[0]
    result[:rows, :] = (one[...] + came[:rows, :].astype(F32)).astype(BF)
    result[rows:, :] = (two[...] + came[rows:, :].astype(F32)).astype(BF)


def sum_pair_job(one, two, came):
    return (sum_pair_kernel, [full(one), full(two), full(came)], [out(came.shape, BF)], {})


def rows_fold_kernel(pos, kept, came, stay, away):
    rows = stay.shape[0]
    for ref, span in ((stay, slice(0, rows)), (away, slice(rows, 2 * rows))):
        ref[...] = (kept[span, :] + came[span, :].astype(F32)).astype(ref.dtype)


def rows_fold_job(kept, came):
    shape = (kept.shape[0] // 2, kept.shape[1])
    return (rows_fold_kernel, [full(kept), full(came)], [out(shape, F32), out(shape, BF)], {})


def line_sum_job(kept, came):
    return (sum_kernel, [full(kept), full(came)], [out(kept.shape, BF)], {})


def finish_kernel(pos, total, opposite, result):
    half = total.shape[0]
    result[pl.ds(pl.multiple_of(pos[3] * half, half), half), :] = total[...]
    result[pl.ds(pl.multiple_of((1 - pos[3]) * half, half), half), :] = opposite[...]


def finish_job(total, opposite):
    shape = (total.shape[0] * 2, total.shape[1])
    return (finish_kernel, [full(total), full(opposite)], [out(shape, BF)], {})


def weight_kernel(norm, pos, sums, line, far, away, kept):
    half = sums.shape[2] // 2
    rows = line.shape[0]
    place = jnp.where(pos[3] == 0, pos[1], pos[2])
    for ref, index in ((away, 1 - place), (kept, place)):
        columns = pl.ds(pl.multiple_of(index * half, 128), half)
        total = dot(sums[0, :rows, columns], line[...], ((0,), (0,)))
        total = total + dot(sums[0, rows:, columns], far[...], ((0,), (0,)))
        ref[0] = (norm * total).astype(ref.dtype)


def weight_terms(pos, sums, line, far, chunk, norm, after):
    groups, _, width = sums.shape
    span = width // CHUNKS
    shape = (groups, width // 2, span)
    flat = lambda array: (array, (array.shape[0], span), lambda s, pos: (0, chunk))
    block = ((1,) + shape[1:], lambda s, pos: (s, 0, 0))
    return call(
        "weight_terms",
        functools.partial(weight_kernel, norm),
        pos,
        [by_rel(sums), flat(line), flat(far)],
        [(shape, BF) + block, (shape, F32) + block],
        grid=(groups,),
        after=after,
        limit=24,
    )


PLACES = (
    lambda pos: jnp.where(pos[3] == 0, pos[2], pos[1]),
    lambda pos: pos[0] % 2,
    lambda pos: pos[0] // 2,
)


def weight_fold_kernel(place, pos, kept, came, stay, away):
    rows = stay.shape[1]
    for ref, index in ((stay, place(pos)), (away, 1 - place(pos))):
        span = pl.ds(pl.multiple_of(index * rows, 16), rows)
        ref[...] = (kept[:, span, :] + came[:, span, :].astype(F32)).astype(ref.dtype)


def weight_fold_job(kept, came, place):
    shape = (kept.shape[0], kept.shape[1] // 2, kept.shape[2])
    return (
        functools.partial(weight_fold_kernel, place),
        [full(kept), full(came)],
        [out(shape, F32), out(shape, BF)],
        {},
    )


def assemble_kernel(pos, *refs):
    result = refs[-1]
    z, y, x, core = pos[0], pos[1], pos[2], pos[3]
    first = jnp.where(core == 0, y, x)
    second = jnp.where(core == 0, x, y)
    count = pl.num_programs(0)
    rows = result.shape[1] // NODES_HERE
    for number, ref in enumerate(refs[:-1]):
        chunk, flip_a = number // 2, number % 2
        span = ref.shape[1]
        for index in range(2 * DEPTH):
            flip_b, k = index // DEPTH, LINE[index % DEPTH]
            block = ((first ^ flip_a) * 2 + (second ^ flip_b)) * DEPTH + z % 2 * 2 + z // 2
            place = block ^ (k % 2 * 2 + k // 2)
            start = (index * count + pl.program_id(0)) * rows
            result[
                0, pl.ds(pl.multiple_of(place * rows, 16), rows), chunk * span : (chunk + 1) * span
            ] = ref[pl.ds(pl.multiple_of(start, 16), rows), :].astype(F32)


def assemble(pos, pieces, groups, width):
    return call(
        "assemble",
        assemble_kernel,
        pos,
        [full(piece) for piece in pieces],
        [out_by_rel(groups, width, width, F32)],
        grid=(groups,),
        limit=24,
    )[0]


def body(
    features, history, history_mean, weights, source_rows, target_owner, target_rows, cotangent
):
    groups, width, _ = weights.shape
    batch = history_mean.shape[1]
    nodes = features.shape[0]
    msgs = source_rows.shape[1]
    owners = lax.axis_size("node")
    scale = 1.0 / (msgs // batch)
    dst = target_owner[:, :, 0] * batch + target_rows
    if owners != NODES_HERE:
        return anywhere(
            features, history, history_mean, weights, source_rows, dst, cotangent, scale
        )
    norm = (batch * owners) ** -0.5
    node = lax.axis_index("node")
    core = lax.axis_index("rel")
    z = node // 4
    pos = jnp.stack([z, node // 2 % 2, node % 2, core]).astype(jnp.int32)
    half = batch // 2
    swap = lambda array: hop(array, CORES)
    numbers = jnp.stack(
        [target_owner[:, :, 0], target_rows, source_rows % PART, source_rows // PART], axis=1
    )
    numbers = numbers.reshape(groups * FIELDS, msgs).astype(BF)
    numbers = jnp.concatenate([numbers, jnp.zeros((EXTRA - groups * FIELDS, msgs), BF)])

    own, theirs, mine = prepare(pos, features, history, numbers, cotangent)
    near_a, near_b = hop(own, FIRST), hop(own, SECOND)
    line_2 = hop(mine, ALONG[2])
    collect = functools.partial(gather, pos, groups, msgs)
    one = collect([own, theirs], [0, 0], [mine])
    (near,), (pair,), (near_b,) = together(
        pos, [join_job([near_a, near_b]), join_job([mine, line_2]), (copy_kernel, [full(near_b)], [out(near_b.shape, BF)], {})], [one]
    )
    near_ab, near_o, line_1 = hop(near_b, FIRST), swap(near), hop(pair, ALONG[1])
    two = collect([near_a, near_o, near_b, near_o], [0, 1, 0, 0], [near_b])
    ((near_ab,),) = together(pos, [gate_job([near_ab])], [two])
    far_ab = swap(near_ab)
    sums = aggregate_near(
        pos, history_mean, [own, near_a, near_b], [one, two], scale, [near_ab]
    )
    ((line,),) = together(pos, [join_job([pair, line_1])], [sums, far_ab])
    far = swap(line)
    sums = aggregate(pos, msgs, batch, near_ab, far_ab, sums, scale, [line])
    plane = [own, near_a, near_b, near_ab]

    chunks = [{"index": index} for index in range(CHUNKS)]
    last = sums
    for chunk in chunks:
        chunk["away"], chunk["kept"] = weight_terms(
            pos, sums, line, far, chunk["index"], norm, [last]
        )
        last = chunk["away"]
        chunk["came"] = hop(chunk["away"], FIRST)
        if chunk["index"] == 0:
            theirs = output_terms(pos, sums, weights, 1, BF, [last])
            last = output = output_terms(pos, sums, weights, 0, F32, [theirs])
    state, grown, given = {"away": theirs, "kept": output}, {}, {}
    ways = (SECOND, ALONG[1], ALONG[2])

    def weight_step(chunk, step):
        if step < 3:

            def sent(kept, away):
                chunk["kept"], chunk["came"] = kept, hop(away, ways[step])

            return weight_fold_job(chunk["kept"], chunk["came"], PLACES[step]), sent
        if step == 3:

            def summed(total):
                total = total.reshape(-1, total.shape[2])
                chunk["line"] = [total, hop(total, ALONG[2])]

            return line_sum_job(chunk["kept"], chunk["came"]), summed

        def joined(line):
            chunk["line"] = [line, hop(line, (ALONG[1], SECOND, FIRST)[step - 4])]

        return join_job(chunk["line"]), joined

    def rows_step(step):
        if step == 0:
            return gate_job([state["away"]]), lambda away: state.update(rows=swap(away))
        if step < 3:

            def sent(kept, away):
                state.update(kept=kept, rows=hop(away, ways[step]))

            return rows_fold_job(state["kept"], state["rows"]), sent
        if step == 3:
            job = line_sum_job(state["kept"], state["rows"])
            return job, lambda total: state.update(total=total, opposite=swap(total))
        job = finish_job(state["total"], state["opposite"])
        return job, lambda rows: state.update(out=rows)

    def back_step(step):
        if step == 0:
            job = join_job([given[2], given[3]])
            return job, lambda away: state.update(far=swap(away))
        if step == 1:
            return gate_job([given[1]]), lambda away: state.update(far_2=swap(away))
        if step == 2:
            job = sum_pair_job(grown[1], grown[3], state["far"])
            return job, lambda away: state.update(first=hop(away, FIRST))
        if step == 3:
            job = sum_rows_job([(grown[2], 0), (state["far_2"], 0), (state["first"], 1)], BF)
            return job, lambda away: state.update(second=hop(away, SECOND))
        if step == 4:
            return gate_job([given[0]]), lambda away: state.update(far_0=swap(away))
        if step == 5:
            terms = [(grown[0], 0), (state["far_0"], 0), (state["first"], 0), (state["second"], 0)]
            job = sum_rows_job(terms, BF)
            return job, lambda own: state.update(own=own, own_o=swap(own))
        job = finish_job(state["own"], state["own_o"])
        return job, lambda rows: state.update(back=rows)

    for steps, covers in ROUNDS:
        planned = []
        for what, step in steps:
            if what == "rows":
                planned.append(rows_step(step))
            elif what == "back":
                planned.append(back_step(step))
            else:
                planned.append(weight_step(chunks[what], step))
        results = together(pos, [job for job, _ in planned], [last])
        for (_, then), result in zip(planned, results):
            then(*result)
        last = results[0][0]
        for cover in covers:
            grown[cover], given[cover] = back_terms(
                pos, batch, msgs, plane[cover], line, far, weights, scale, [last]
            )
            last = grown[cover]
    pieces = [piece for chunk in chunks for piece in chunk["line"]]
    return state["out"], assemble(pos, pieces, groups, width), state["back"]


def anywhere(features, history, history_mean, weights, source_rows, dst, cotangent, scale):
    groups, width, _ = weights.shape
    batch, nodes = cotangent.shape[0], features.shape[0]
    total_batch = batch * lax.axis_size("node")
    deltas = (features.astype(F32) - history.astype(F32)).astype(BF)
    every = lax.all_gather(cotangent, "node", tiled=True)
    out = jnp.zeros((total_batch, width), F32)
    local = jnp.zeros((batch, width), F32)
    terms = jnp.zeros((nodes, width), F32)
    grads = []
    for rel in range(groups):
        rows = jnp.take(deltas, source_rows[rel], axis=0)
        picked = jnp.take(every, dst[rel], axis=0)
        out = out.at[dst[rel]].add(scale * dot(rows, weights[rel]))
        local = local + dot(history_mean[rel], weights[rel])
        edge = (scale * dot(picked, weights[rel], ((1,), (1,)))).astype(BF)
        terms = terms.at[source_rows[rel]].add(edge.astype(F32))
        grads.append(
            dot(history_mean[rel], cotangent, ((0,), (0,)))
            + scale * dot(rows, picked, ((0,), (0,)))
        )
    layer_out = lax.psum(lax.psum_scatter(out, "node", tiled=True) + local, "rel").astype(BF)
    weight_grads = lax.psum(jnp.stack(grads) * total_batch**-0.5, "node")
    return layer_out, weight_grads, lax.psum(terms, "rel").astype(BF)


def solution(mesh):
    in_specs = (
        P("node", None),
        P("node", None),
        P("rel", "node", None),
        P("rel", None, None),
        P("rel", "node"),
        P("rel", "node", None),
        P("rel", "node"),
        P("node", None),
    )
    out_specs = (P("node", None), P("rel", None, None), P("node", None))
    return jax.shard_map(body, mesh=mesh, in_specs=in_specs, out_specs=out_specs, check_vma=False)
```

```python
import functools

import jax
import jax.numpy as jnp
from jax import lax
from jax.experimental import pallas as pl
from jax.experimental.pallas import tpu as pltpu
from jax.sharding import PartitionSpec as P

BF = jnp.bfloat16
F32 = jnp.float32
AXES = ("node", "rel")
DEPTH, SIDE = 4, 2
CHUNKS = 2
LIMIT = 24
ROUNDS = (
    (((0, 0),), (2,)),
    (((1, 0), (0, 1),), (3,)),
    (((0, 2), (1, 1), ("back", 0), ("rows", 0),), (1,)),
    (((0, 3), (1, 2), ("back", 2), ("back", 1),), (0,)),
    (((0, 4), (1, 3), ("back", 3), ("back", 4), ("rows", 1),), ()),
    (((0, 5), (1, 4), ("back", 5),), ()),
    (((1, 5), ("back", 6), ("rows", 2),), ()),
    ((("rows", 3),), ()),
    ((("rows", 4),), ()),
)
NODES_HERE = DEPTH * SIDE * SIDE


def dot(a, b, dims=((1,), (0,))):
    return lax.dot_general(a, b, (dims, ((), ())), preferred_element_type=F32)


def call(name, kernel, pos, ins, outs, grid=(1,), after=(), alias=None, limit=24, scratch=()):
    def spec(block, index):
        if block is None:
            return pl.BlockSpec(memory_space=pl.ANY)
        if index is None:
            return pl.BlockSpec(block, lambda *_: (0,) * len(block))
        return pl.BlockSpec(block, index)

    many = len(ins)

    def run(pos_ref, *refs):
        kernel(pos_ref, *refs[:many], *refs[many + len(after) :])

    return pl.pallas_call(
        run,
        grid_spec=pltpu.PrefetchScalarGridSpec(
            num_scalar_prefetch=1,
            grid=grid,
            in_specs=[spec(block, index) for _, block, index in ins]
            + [pl.BlockSpec(memory_space=pl.ANY)] * len(after),
            out_specs=[spec(block, index) for _, _, block, index in outs],
            scratch_shapes=scratch,
        ),
        out_shape=[jax.ShapeDtypeStruct(shape, dtype) for shape, dtype, _, _ in outs],
        input_output_aliases=alias or {},
        compiler_params=pltpu.CompilerParams(
            dimension_semantics=("arbitrary",) * len(grid), vmem_limit_bytes=limit * 1024 * 1024
        ),
        cost_estimate=pl.CostEstimate(flops=1000, bytes_accessed=1000, transcendentals=0),
        name=name,
    )(pos, *[array for array, _, _ in ins], *after)


def full(array):
    return (array, array.shape, None)


def out(shape, dtype):
    return (shape, dtype, shape, None)


def together(pos, jobs, after):
    ins = [entry for _, job_ins, _, _ in jobs for entry in job_ins]
    outs = [entry for _, _, job_outs, _ in jobs for entry in job_outs]
    spans, alias, i, o = [], {}, 0, 0
    for _, job_ins, job_outs, job_alias in jobs:
        spans.append((i, i + len(job_ins), o, o + len(job_outs)))
        alias.update({1 + i + source: o + target for source, target in job_alias.items()})
        i, o = spans[-1][1], spans[-1][3]

    def kernel(pos_ref, *refs):
        for (work, _, _, _), (a, b, c, d) in zip(jobs, spans):
            work(pos_ref, *refs[a:b], *refs[len(ins) + c : len(ins) + d])

    results = call("step", kernel, pos, ins, outs, after=after, alias=alias, limit=LIMIT)
    return [results[c:d] for _, _, c, d in spans]


def gate_job(arrays):
    return (
        lambda *_: None,
        [(array, None, None) for array in arrays],
        [(array.shape, array.dtype, None, None) for array in arrays],
        {i: i for i in range(len(arrays))},
    )


def pairs(move):
    listed = []
    for node in range(NODES_HERE):
        for core in range(2):
            z, y, x = node // 4, node // 2 % 2, node % 2
            tz, ty, tx, tc = move(z, y, x, core)
            listed.append((node * 2 + core, (tz * 4 + ty * 2 + tx) * 2 + tc))
    return listed


FIRST = pairs(lambda z, y, x, c: (z, y ^ (1 - c), x ^ c, c))
SECOND = pairs(lambda z, y, x, c: (z, y ^ c, x ^ (1 - c), c))
ALONG = [pairs(lambda z, y, x, c, k=k: (z ^ k, y, x, c)) for k in range(DEPTH)]
LINE = (0, 2, 1, 3)
CORES = pairs(lambda z, y, x, c: (z, y, x, 1 - c))


def hop(array, table):
    return lax.ppermute(array, AXES, table)


def by_rel(array):
    return (array, (1,) + array.shape[1:], lambda r, pos: (r, 0, 0))


def out_by_rel(groups, rows, width, dtype):
    return ((groups, rows, width), dtype, (1, rows, width), lambda r, pos: (r, 0, 0))


def join_kernel(pos, *refs):
    start = 0
    for ref in refs[:-1]:
        refs[-1][start : start + ref.shape[0], :] = ref[...]
        start += ref.shape[0]


def copy_kernel(pos, source, target):
    target[...] = source[...]


def join_job(pieces):
    shape = (sum(piece.shape[0] for piece in pieces), pieces[0].shape[1])
    return (join_kernel, [full(piece) for piece in pieces], [out(shape, BF)], {})


def one_hot(values, places):
    return (values == places).astype(F32).astype(BF)


def partial_step(pos, core, first, second, batch, dst, sent, local):
    half = batch // 2
    rows = lax.broadcasted_iota(jnp.int32, (half, dst.shape[1]), 0)
    hot = []
    for depth in LINE:
        base = owner_of(pos, core, first, second, depth) * batch + core * half
        hot.append(one_hot(dst[...] - base, rows))
    total = dot(jnp.concatenate(hot, axis=0), sent[...])
    own = local[pl.ds(pl.multiple_of(core * half, half), half), :]
    here = (first + second == 0).astype(F32)
    return jnp.concatenate([total[:half] + here * own, total[half:]], axis=0)


def one_hot(values, places):
    return (values == places).astype(F32).astype(BF)


FIELDS = 4
EXTRA = 16
PART = 256


def fields(block, rel, count):
    places = lax.broadcasted_iota(jnp.int32, block.shape, 0)
    rows = [
        jnp.sum(jnp.where(places == rel * FIELDS + f, block, 0.0), axis=0, keepdims=True)
        for f in range(FIELDS)
    ]
    return [row[:, :count].astype(jnp.int32) for row in rows]


def prepare_kernel(pos, feat, hist, numbers, cot, mine, theirs, line):
    half = feat.shape[0] // 2
    for ref, core in ((mine, pos[3]), (theirs, 1 - pos[3])):
        span = pl.ds(pl.multiple_of(core * half, half), half)
        deltas = feat[span, :].astype(F32) - hist[span, :].astype(F32)
        ref[:half, :] = deltas.astype(BF)
        ref[half:, :] = jnp.zeros((EXTRA, ref.shape[1]), BF)
        ref[half:, : numbers.shape[1]] = numbers[...]
    half = line.shape[0]
    line[...] = cot[pl.ds(pl.multiple_of(pos[3] * half, half), half), :]


def prepare(pos, features, history, numbers, cot):
    nodes, width = features.shape
    shape = (nodes // 2 + EXTRA, width)
    return call(
        "prepare",
        prepare_kernel,
        pos,
        [full(features), full(history), full(numbers), full(cot)],
        [out(shape, BF), out(shape, BF), out((cot.shape[0] // 2, width), BF)],
        limit=24,
    )


def gather_step(pos, rel, msgs, mine, theirs):
    half = mine.shape[0] - EXTRA
    _, _, low, high = fields(mine[half:, :].astype(F32), rel, msgs)
    column = jnp.transpose(jnp.broadcast_to(low + PART * high, (128, msgs)))
    lanes = lax.broadcasted_iota(jnp.int32, (msgs, 128), 1)
    total = None
    for ref, core in ((mine, pos[3]), (theirs, 1 - pos[3])):
        hot = [one_hot(column, lanes + (core * half + n)) for n in range(0, half, 128)]
        term = dot(jnp.concatenate(hot, axis=1), ref[:half, :])
        total = term if total is None else total + term
    return total.astype(BF)


def gather_kernel(msgs, pos, *refs):
    result = refs[-1]
    for n in range(len(refs) // 2):
        result[0, n * msgs : (n + 1) * msgs, :] = gather_step(
            pos, pl.program_id(0), msgs, refs[2 * n], refs[2 * n + 1]
        )


def gather(pos, groups, msgs, pieces, places, after):
    rows, width = pieces[0].shape
    return call(
        "gather",
        functools.partial(gather_kernel, msgs),
        pos,
        [
            (piece, (rows, width), lambda r, pos, place=place: (place, 0))
            for piece, place in zip(pieces, places)
        ],
        [out_by_rel(groups, len(pieces) // 2 * msgs, width, BF)],
        grid=(groups,),
        after=after,
        limit=24,
    )[0]


def bases(pos, batch):
    half = batch // 2
    for core in (pos[3], 1 - pos[3]):
        for depth in LINE:
            owner = (pos[0] ^ depth) * SIDE * SIDE + pos[1] * SIDE + pos[2]
            yield owner * batch + core * half


def aggregate_part(scale, pos, batch, payloads, moved, side):
    rel = pl.program_id(0)
    half = batch // 2
    msgs = moved.shape[0] // len(payloads)
    dst = []
    for ref in payloads:
        owner, row, _, _ = fields(ref[ref.shape[0] - EXTRA :, :].astype(F32), rel, msgs)
        dst.append(owner * batch + row)
    dst = jnp.concatenate(dst, axis=1)
    rows = lax.broadcasted_iota(jnp.int32, (half, dst.shape[1]), 0)
    places = list(bases(pos, batch))[side * DEPTH : (side + 1) * DEPTH]
    hot = [one_hot(dst - base, rows) for base in places]
    return scale * dot(jnp.concatenate(hot, axis=0), moved)


def aggregate_near_kernel(scale, pos, own, near_a, near_b, one, two, mean, result):
    batch = mean.shape[1]
    half = batch // 2
    moved = jnp.concatenate([one[0], two[0]], axis=0)
    for side in range(2):
        total = aggregate_part(scale, pos, batch, [own, near_a, near_b], moved, side)
        core = pos[3] if side == 0 else 1 - pos[3]
        own_mean = mean[0, pl.ds(pl.multiple_of(core * half, half), half), :].astype(F32)
        at = side * DEPTH * half
        result[0, at : at + half, :] = total[:half] + own_mean
        result[0, at + half : at + DEPTH * half, :] = total[half:]


def aggregate_near(pos, mean, payloads, moved, scale, after):
    groups, batch, width = mean.shape
    return call(
        "aggregate_near",
        functools.partial(aggregate_near_kernel, scale),
        pos,
        [full(p) for p in payloads] + [by_rel(m) for m in moved] + [by_rel(mean)],
        [out_by_rel(groups, DEPTH * batch, width, F32)],
        grid=(groups,),
        after=after,
        limit=32,
    )[0]


def aggregate_kernel(scale, msgs, batch, pos, near_ab, far_ab, before, result):
    moved = gather_step(pos, pl.program_id(0), msgs, near_ab, far_ab)
    rows = DEPTH * batch // 2
    for side in range(2):
        span = slice(side * rows, (side + 1) * rows)
        total = aggregate_part(scale, pos, batch, [near_ab], moved, side)
        result[0, span, :] = (total + before[0, span, :]).astype(BF)


def aggregate(pos, msgs, batch, near_ab, far_ab, before, scale, after):
    groups, rows, width = before.shape
    return call(
        "aggregate",
        functools.partial(aggregate_kernel, scale, msgs, batch),
        pos,
        [full(near_ab), full(far_ab), by_rel(before)],
        [out_by_rel(groups, rows, width, BF)],
        grid=(groups,),
        after=after,
        limit=32,
    )[0]


def output_kernel(pos, sums, weight, result):
    total = dot(sums[0], weight[0])
    for rel in range(1, sums.shape[0]):
        total = total + dot(sums[rel], weight[rel])
    result[...] = total.astype(result.dtype)


def output_terms(pos, sums, weights, side, dtype, after):
    groups, rows, width = sums.shape
    return call(
        "output_terms",
        output_kernel,
        pos,
        [(sums, (groups, rows // 2, width), lambda s, pos: (0, side, 0)), full(weights)],
        [out((rows // 2, width), dtype)],
        after=after,
        limit=24,
    )[0]


def back_kernel(scale, batch, msgs, pos, payload, line, far, weight, kept, away, total):
    rel = pl.program_id(0)
    half = line.shape[0] // DEPTH
    owner, row, low, high = fields(
        payload[payload.shape[0] - EXTRA :, :].astype(F32), rel, msgs
    )
    column = jnp.transpose(jnp.broadcast_to(owner * batch + row, (128, msgs)))
    lanes = lax.broadcasted_iota(jnp.int32, (msgs, half), 1)
    hot = [one_hot(column, lanes + base) for base in bases(pos, batch)]
    picked = dot(jnp.concatenate(hot[:DEPTH], axis=1), line[...])
    picked = picked + dot(jnp.concatenate(hot[DEPTH:], axis=1), far[...])
    grads = (scale * dot(picked.astype(BF), weight[0], ((1,), (1,)))).astype(BF)
    rows = lax.broadcasted_iota(jnp.int32, (total.shape[0], msgs), 0)
    term = dot(one_hot(low + PART * high, rows), grads)

    @pl.when(rel == 0)
    def _():
        total[...] = term

    @pl.when(rel > 0)
    def _():
        total[...] += term

    @pl.when(rel == pl.num_programs(0) - 1)
    def _():
        size = kept.shape[0]
        kept[...] = total[pl.ds(pl.multiple_of(pos[3] * size, size), size), :]
        away[...] = total[pl.ds(pl.multiple_of((1 - pos[3]) * size, size), size), :].astype(BF)


def back_terms(pos, batch, msgs, payload, line, far, weights, scale, after):
    groups, width, _ = weights.shape
    half = payload.shape[0] - EXTRA
    return call(
        "feature_terms",
        functools.partial(back_kernel, scale, batch, msgs),
        pos,
        [full(payload), full(line), full(far), by_rel(weights)],
        [out((half, width), F32), out((half, width), BF)],
        grid=(groups,),
        after=after,
        scratch=[pltpu.VMEM((2 * half, width), F32)],
        limit=24,
    )


def sum_kernel(pos, *refs):
    total = refs[0][...].astype(F32)
    for ref in refs[1:-1]:
        total = total + ref[...].astype(F32)
    refs[-1][...] = total.astype(refs[-1].dtype)


def sum_rows_job(terms, dtype):
    shape = terms[0][0].shape
    ins = [(array, shape, lambda s, pos, place=place: (place, 0)) for array, place in terms]
    return (sum_kernel, ins, [out(shape, dtype)], {})


def sum_pair_kernel(pos, one, two, came, result):
    rows = one.shape[0]
    result[:rows, :] = (one[...] + came[:rows, :].astype(F32)).astype(BF)
    result[rows:, :] = (two[...] + came[rows:, :].astype(F32)).astype(BF)


def sum_pair_job(one, two, came):
    return (sum_pair_kernel, [full(one), full(two), full(came)], [out(came.shape, BF)], {})


def rows_fold_kernel(pos, kept, came, stay, away):
    rows = stay.shape[0]
    for ref, span in ((stay, slice(0, rows)), (away, slice(rows, 2 * rows))):
        ref[...] = (kept[span, :] + came[span, :].astype(F32)).astype(ref.dtype)


def rows_fold_job(kept, came):
    shape = (kept.shape[0] // 2, kept.shape[1])
    return (rows_fold_kernel, [full(kept), full(came)], [out(shape, F32), out(shape, BF)], {})


def line_sum_job(kept, came):
    return (sum_kernel, [full(kept), full(came)], [out(kept.shape, BF)], {})


def finish_kernel(pos, total, opposite, result):
    half = total.shape[0]
    result[pl.ds(pl.multiple_of(pos[3] * half, half), half), :] = total[...]
    result[pl.ds(pl.multiple_of((1 - pos[3]) * half, half), half), :] = opposite[...]


def finish_job(total, opposite):
    shape = (total.shape[0] * 2, total.shape[1])
    return (finish_kernel, [full(total), full(opposite)], [out(shape, BF)], {})


def weight_kernel(norm, pos, sums, line, far, away, kept):
    half = sums.shape[2] // 2
    rows = line.shape[0]
    place = jnp.where(pos[3] == 0, pos[1], pos[2])
    for ref, index in ((away, 1 - place), (kept, place)):
        columns = pl.ds(pl.multiple_of(index * half, 128), half)
        total = dot(sums[0, :rows, columns], line[...], ((0,), (0,)))
        total = total + dot(sums[0, rows:, columns], far[...], ((0,), (0,)))
        ref[0] = (norm * total).astype(ref.dtype)


def weight_terms(pos, sums, line, far, chunk, norm, after):
    groups, _, width = sums.shape
    span = width // CHUNKS
    shape = (groups, width // 2, span)
    flat = lambda array: (array, (array.shape[0], span), lambda s, pos: (0, chunk))
    block = ((1,) + shape[1:], lambda s, pos: (s, 0, 0))
    return call(
        "weight_terms",
        functools.partial(weight_kernel, norm),
        pos,
        [by_rel(sums), flat(line), flat(far)],
        [(shape, BF) + block, (shape, F32) + block],
        grid=(groups,),
        after=after,
        limit=24,
    )


PLACES = (
    lambda pos: jnp.where(pos[3] == 0, pos[2], pos[1]),
    lambda pos: pos[0] % 2,
)


def weight_fold_kernel(place, pos, kept, came, stay, away):
    rows = stay.shape[1]
    for ref, index in ((stay, place(pos)), (away, 1 - place(pos))):
        span = pl.ds(pl.multiple_of(index * rows, 16), rows)
        ref[...] = (kept[:, span, :] + came[:, span, :].astype(F32)).astype(ref.dtype)


def weight_fold_job(kept, came, place):
    shape = (kept.shape[0], kept.shape[1] // 2, kept.shape[2])
    return (
        functools.partial(weight_fold_kernel, place),
        [full(kept), full(came)],
        [out(shape, F32), out(shape, BF)],
        {},
    )


def assemble_kernel(pos, *refs):
    result = refs[-1]
    z, y, x, core = pos[0], pos[1], pos[2], pos[3]
    first = jnp.where(core == 0, y, x)
    second = jnp.where(core == 0, x, y)
    count = pl.num_programs(0)
    rows = result.shape[1] // (2 * SIDE * SIDE)
    for number, ref in enumerate(refs[:-1]):
        chunk, flip_a = number // 2, number % 2
        span = ref.shape[1]
        for index in range(4):
            flip_b, flip_z = index // 2, index % 2
            place = ((first ^ flip_a) * 2 + (second ^ flip_b)) * 2 + (z % 2 ^ flip_z)
            start = (index * count + pl.program_id(0)) * rows
            result[
                0, pl.ds(pl.multiple_of(place * rows, 16), rows), chunk * span : (chunk + 1) * span
            ] = ref[pl.ds(pl.multiple_of(start, 16), rows), :].astype(F32)


def assemble(pos, pieces, groups, width):
    return call(
        "assemble",
        assemble_kernel,
        pos,
        [full(piece) for piece in pieces],
        [out_by_rel(groups, width, width, F32)],
        grid=(groups,),
        limit=24,
    )[0]


def body(
    features, history, history_mean, weights, source_rows, target_owner, target_rows, cotangent
):
    groups, width, _ = weights.shape
    batch = history_mean.shape[1]
    nodes = features.shape[0]
    msgs = source_rows.shape[1]
    owners = lax.axis_size("node")
    scale = 1.0 / (msgs // batch)
    dst = target_owner[:, :, 0] * batch + target_rows
    if owners != NODES_HERE:
        return anywhere(
            features, history, history_mean, weights, source_rows, dst, cotangent, scale
        )
    norm = (batch * owners) ** -0.5
    node = lax.axis_index("node")
    core = lax.axis_index("rel")
    z = node // 4
    pos = jnp.stack([z, node // 2 % 2, node % 2, core]).astype(jnp.int32)
    half = batch // 2
    swap = lambda array: hop(array, CORES)
    numbers = jnp.stack(
        [target_owner[:, :, 0], target_rows, source_rows % PART, source_rows // PART], axis=1
    )
    numbers = numbers.reshape(groups * FIELDS, msgs).astype(BF)
    numbers = jnp.concatenate([numbers, jnp.zeros((EXTRA - groups * FIELDS, msgs), BF)])

    own, theirs, mine = prepare(pos, features, history, numbers, cotangent)
    near_a, near_b = hop(own, FIRST), hop(own, SECOND)
    line_2 = hop(mine, ALONG[2])
    collect = functools.partial(gather, pos, groups, msgs)
    one = collect([own, theirs], [0, 0], [mine])
    (near,), (pair,), (near_b,) = together(
        pos, [join_job([near_a, near_b]), join_job([mine, line_2]), (copy_kernel, [full(near_b)], [out(near_b.shape, BF)], {})], [one]
    )
    near_ab, near_o, line_1 = hop(near_b, FIRST), swap(near), hop(pair, ALONG[1])
    two = collect([near_a, near_o, near_b, near_o], [0, 1, 0, 0], [near_b])
    ((near_ab,),) = together(pos, [gate_job([near_ab])], [two])
    far_ab = swap(near_ab)
    sums = aggregate_near(
        pos, history_mean, [own, near_a, near_b], [one, two], scale, [near_ab]
    )
    ((line,),) = together(pos, [join_job([pair, line_1])], [sums, far_ab])
    far = swap(line)
    sums = aggregate(pos, msgs, batch, near_ab, far_ab, sums, scale, [line])
    plane = [own, near_a, near_b, near_ab]

    chunks = [{"index": index} for index in range(CHUNKS)]
    last = sums
    for chunk in chunks:
        chunk["away"], chunk["kept"] = weight_terms(
            pos, sums, line, far, chunk["index"], norm, [last]
        )
        last = chunk["away"]
        chunk["came"] = hop(chunk["away"], FIRST)
        if chunk["index"] == 0:
            theirs = output_terms(pos, sums, weights, 1, BF, [last])
            last = output = output_terms(pos, sums, weights, 0, F32, [theirs])
    state, grown, given = {"away": theirs, "kept": output}, {}, {}
    ways = (SECOND, ALONG[1], ALONG[2])

    def weight_step(chunk, step):
        if step < 2:

            def sent(kept, away):
                chunk["kept"], chunk["came"] = kept, hop(away, ways[step])

            return weight_fold_job(chunk["kept"], chunk["came"], PLACES[step]), sent
        if step == 2:
            def exchanged(total):
                chunk["kept"], chunk["came"] = total, hop(total, ALONG[2])

            return line_sum_job(chunk["kept"], chunk["came"]), exchanged
        if step == 3:

            def summed(total):
                total = total.reshape(-1, total.shape[2])
                chunk["line"] = [total, hop(total, ALONG[1])]

            return line_sum_job(chunk["kept"], chunk["came"]), summed

        def joined(line):
            chunk["line"] = [line, hop(line, (SECOND, FIRST)[step - 4])]

        return join_job(chunk["line"]), joined

    def rows_step(step):
        if step == 0:
            return gate_job([state["away"]]), lambda away: state.update(rows=swap(away))
        if step < 3:

            def sent(kept, away):
                state.update(kept=kept, rows=hop(away, ways[step]))

            return rows_fold_job(state["kept"], state["rows"]), sent
        if step == 3:
            job = line_sum_job(state["kept"], state["rows"])
            return job, lambda total: state.update(total=total, opposite=swap(total))
        job = finish_job(state["total"], state["opposite"])
        return job, lambda rows: state.update(out=rows)

    def back_step(step):
        if step == 0:
            job = join_job([given[2], given[3]])
            return job, lambda away: state.update(far=swap(away))
        if step == 1:
            return gate_job([given[1]]), lambda away: state.update(far_2=swap(away))
        if step == 2:
            job = sum_pair_job(grown[1], grown[3], state["far"])
            return job, lambda away: state.update(first=hop(away, FIRST))
        if step == 3:
            job = sum_rows_job([(grown[2], 0), (state["far_2"], 0), (state["first"], 1)], BF)
            return job, lambda away: state.update(second=hop(away, SECOND))
        if step == 4:
            return gate_job([given[0]]), lambda away: state.update(far_0=swap(away))
        if step == 5:
            terms = [(grown[0], 0), (state["far_0"], 0), (state["first"], 0), (state["second"], 0)]
            job = sum_rows_job(terms, BF)
            return job, lambda own: state.update(own=own, own_o=swap(own))
        job = finish_job(state["own"], state["own_o"])
        return job, lambda rows: state.update(back=rows)

    for steps, covers in ROUNDS:
        planned = []
        for what, step in steps:
            if what == "rows":
                planned.append(rows_step(step))
            elif what == "back":
                planned.append(back_step(step))
            else:
                planned.append(weight_step(chunks[what], step))
        results = together(pos, [job for job, _ in planned], [last])
        for (_, then), result in zip(planned, results):
            then(*result)
        last = results[0][0]
        for cover in covers:
            grown[cover], given[cover] = back_terms(
                pos, batch, msgs, plane[cover], line, far, weights, scale, [last]
            )
            last = grown[cover]
    pieces = [piece for chunk in chunks for piece in chunk["line"]]
    return state["out"], assemble(pos, pieces, groups, width), state["back"]


def anywhere(features, history, history_mean, weights, source_rows, dst, cotangent, scale):
    groups, width, _ = weights.shape
    batch, nodes = cotangent.shape[0], features.shape[0]
    total_batch = batch * lax.axis_size("node")
    deltas = (features.astype(F32) - history.astype(F32)).astype(BF)
    every = lax.all_gather(cotangent, "node", tiled=True)
    out = jnp.zeros((total_batch, width), F32)
    local = jnp.zeros((batch, width), F32)
    terms = jnp.zeros((nodes, width), F32)
    grads = []
    for rel in range(groups):
        rows = jnp.take(deltas, source_rows[rel], axis=0)
        picked = jnp.take(every, dst[rel], axis=0)
        out = out.at[dst[rel]].add(scale * dot(rows, weights[rel]))
        local = local + dot(history_mean[rel], weights[rel])
        edge = (scale * dot(picked, weights[rel], ((1,), (1,)))).astype(BF)
        terms = terms.at[source_rows[rel]].add(edge.astype(F32))
        grads.append(
            dot(history_mean[rel], cotangent, ((0,), (0,)))
            + scale * dot(rows, picked, ((0,), (0,)))
        )
    layer_out = lax.psum(lax.psum_scatter(out, "node", tiled=True) + local, "rel").astype(BF)
    weight_grads = lax.psum(jnp.stack(grads) * total_batch**-0.5, "node")
    return layer_out, weight_grads, lax.psum(terms, "rel").astype(BF)


def solution(mesh):
    in_specs = (
        P("node", None),
        P("node", None),
        P("rel", "node", None),
        P("rel", None, None),
        P("rel", "node"),
        P("rel", "node", None),
        P("rel", "node"),
        P("node", None),
    )
    out_specs = (P("node", None), P("rel", None, None), P("node", None))
    return jax.shard_map(body, mesh=mesh, in_specs=in_specs, out_specs=out_specs, check_vma=False)
```

```python
import functools

import jax
import jax.numpy as jnp
from jax import lax
from jax.experimental import pallas as pl
from jax.experimental.pallas import tpu as pltpu
from jax.sharding import PartitionSpec as P

BF = jnp.bfloat16
F32 = jnp.float32
AXES = ("node", "rel")
DEPTH, SIDE = 4, 2
CHUNKS = 2
LIMIT = 24
ROUNDS = (
    (((0, 0),), (2,)),
    (((1, 0), (0, 1),), (3,)),
    (((0, 2), (1, 1), ("back", 0), ("rows", 0),), (1,)),
    (((0, 3), (1, 2), ("back", 2), ("back", 1),), (0,)),
    (((0, 4), (1, 3), ("back", 3), ("back", 4), ("rows", 1),), ()),
    (((0, 5), (1, 4), ("back", 5),), ()),
    (((1, 5), ("back", 6), ("rows", 2),), ()),
    ((("rows", 3),), ()),
    ((("rows", 4),), ()),
)
NODES_HERE = DEPTH * SIDE * SIDE


def dot(a, b, dims=((1,), (0,))):
    return lax.dot_general(a, b, (dims, ((), ())), preferred_element_type=F32)


def call(name, kernel, pos, ins, outs, grid=(1,), after=(), alias=None, limit=24, scratch=()):
    def spec(block, index):
        if block is None:
            return pl.BlockSpec(memory_space=pl.ANY)
        if index is None:
            return pl.BlockSpec(block, lambda *_: (0,) * len(block))
        return pl.BlockSpec(block, index)

    many = len(ins)

    def run(pos_ref, *refs):
        kernel(pos_ref, *refs[:many], *refs[many + len(after) :])

    return pl.pallas_call(
        run,
        grid_spec=pltpu.PrefetchScalarGridSpec(
            num_scalar_prefetch=1,
            grid=grid,
            in_specs=[spec(block, index) for _, block, index in ins]
            + [pl.BlockSpec(memory_space=pl.ANY)] * len(after),
            out_specs=[spec(block, index) for _, _, block, index in outs],
            scratch_shapes=scratch,
        ),
        out_shape=[jax.ShapeDtypeStruct(shape, dtype) for shape, dtype, _, _ in outs],
        input_output_aliases=alias or {},
        compiler_params=pltpu.CompilerParams(
            dimension_semantics=("arbitrary",) * len(grid), vmem_limit_bytes=limit * 1024 * 1024
        ),
        cost_estimate=pl.CostEstimate(flops=1000, bytes_accessed=1000, transcendentals=0),
        name=name,
    )(pos, *[array for array, _, _ in ins], *after)


def full(array):
    return (array, array.shape, None)


def out(shape, dtype):
    return (shape, dtype, shape, None)


def together(pos, jobs, after):
    ins = [entry for _, job_ins, _, _ in jobs for entry in job_ins]
    outs = [entry for _, _, job_outs, _ in jobs for entry in job_outs]
    spans, alias, i, o = [], {}, 0, 0
    for _, job_ins, job_outs, job_alias in jobs:
        spans.append((i, i + len(job_ins), o, o + len(job_outs)))
        alias.update({1 + i + source: o + target for source, target in job_alias.items()})
        i, o = spans[-1][1], spans[-1][3]

    def kernel(pos_ref, *refs):
        for (work, _, _, _), (a, b, c, d) in zip(jobs, spans):
            work(pos_ref, *refs[a:b], *refs[len(ins) + c : len(ins) + d])

    results = call("step", kernel, pos, ins, outs, after=after, alias=alias, limit=LIMIT)
    return [results[c:d] for _, _, c, d in spans]


def gate_job(arrays):
    return (
        lambda *_: None,
        [(array, None, None) for array in arrays],
        [(array.shape, array.dtype, None, None) for array in arrays],
        {i: i for i in range(len(arrays))},
    )


def pairs(move):
    listed = []
    for node in range(NODES_HERE):
        for core in range(2):
            z, y, x = node // 4, node // 2 % 2, node % 2
            tz, ty, tx, tc = move(z, y, x, core)
            listed.append((node * 2 + core, (tz * 4 + ty * 2 + tx) * 2 + tc))
    return listed


FIRST = pairs(lambda z, y, x, c: (z, y ^ (1 - c), x ^ c, c))
SECOND = pairs(lambda z, y, x, c: (z, y ^ c, x ^ (1 - c), c))
ALONG = [pairs(lambda z, y, x, c, k=k: (z ^ k, y, x, c)) for k in range(DEPTH)]
LINE = (0, 2, 1, 3)
CORES = pairs(lambda z, y, x, c: (z, y, x, 1 - c))


def hop(array, table):
    return lax.ppermute(array, AXES, table)


def by_rel(array):
    return (array, (1,) + array.shape[1:], lambda r, pos: (r, 0, 0))


def out_by_rel(groups, rows, width, dtype):
    return ((groups, rows, width), dtype, (1, rows, width), lambda r, pos: (r, 0, 0))


def join_kernel(pos, *refs):
    start = 0
    for ref in refs[:-1]:
        refs[-1][start : start + ref.shape[0], :] = ref[...]
        start += ref.shape[0]


def copy_kernel(pos, source, target):
    target[...] = source[...]


def join_job(pieces):
    shape = (sum(piece.shape[0] for piece in pieces), pieces[0].shape[1])
    return (join_kernel, [full(piece) for piece in pieces], [out(shape, BF)], {})


def one_hot(values, places):
    return (values == places).astype(F32).astype(BF)


def partial_step(pos, core, first, second, batch, dst, sent, local):
    half = batch // 2
    rows = lax.broadcasted_iota(jnp.int32, (half, dst.shape[1]), 0)
    hot = []
    for depth in LINE:
        base = owner_of(pos, core, first, second, depth) * batch + core * half
        hot.append(one_hot(dst[...] - base, rows))
    total = dot(jnp.concatenate(hot, axis=0), sent[...])
    own = local[pl.ds(pl.multiple_of(core * half, half), half), :]
    here = (first + second == 0).astype(F32)
    return jnp.concatenate([total[:half] + here * own, total[half:]], axis=0)


def one_hot(values, places):
    return (values == places).astype(F32).astype(BF)


FIELDS = 4
EXTRA = 16
PART = 256


def fields(block, rel, count):
    places = lax.broadcasted_iota(jnp.int32, block.shape, 0)
    rows = [
        jnp.sum(jnp.where(places == rel * FIELDS + f, block, 0.0), axis=0, keepdims=True)
        for f in range(FIELDS)
    ]
    return [row[:, :count].astype(jnp.int32) for row in rows]


def prepare_kernel(pos, feat, hist, numbers, cot, mine, theirs, line):
    half = feat.shape[0] // 2
    for ref, core in ((mine, pos[3]), (theirs, 1 - pos[3])):
        span = pl.ds(pl.multiple_of(core * half, half), half)
        deltas = feat[span, :].astype(F32) - hist[span, :].astype(F32)
        ref[:half, :] = deltas.astype(BF)
        ref[half:, :] = jnp.zeros((EXTRA, ref.shape[1]), BF)
        ref[half:, : numbers.shape[1]] = numbers[...]
    half = line.shape[0]
    line[...] = cot[pl.ds(pl.multiple_of(pos[3] * half, half), half), :]


def prepare(pos, features, history, numbers, cot):
    nodes, width = features.shape
    shape = (nodes // 2 + EXTRA, width)
    return call(
        "prepare",
        prepare_kernel,
        pos,
        [full(features), full(history), full(numbers), full(cot)],
        [out(shape, BF), out(shape, BF), out((cot.shape[0] // 2, width), BF)],
        limit=24,
    )


def gather_step(pos, rel, msgs, mine, theirs):
    half = mine.shape[0] - EXTRA
    _, _, low, high = fields(mine[half:, :].astype(F32), rel, msgs)
    column = jnp.transpose(jnp.broadcast_to(low + PART * high, (128, msgs)))
    lanes = lax.broadcasted_iota(jnp.int32, (msgs, 128), 1)
    total = None
    for ref, core in ((mine, pos[3]), (theirs, 1 - pos[3])):
        hot = [one_hot(column, lanes + (core * half + n)) for n in range(0, half, 128)]
        term = dot(jnp.concatenate(hot, axis=1), ref[:half, :])
        total = term if total is None else total + term
    return total.astype(BF)


def gather_kernel(msgs, pos, *refs):
    result = refs[-1]
    for n in range(len(refs) // 2):
        result[0, n * msgs : (n + 1) * msgs, :] = gather_step(
            pos, pl.program_id(0), msgs, refs[2 * n], refs[2 * n + 1]
        )


def gather(pos, groups, msgs, pieces, places, after):
    rows, width = pieces[0].shape
    return call(
        "gather",
        functools.partial(gather_kernel, msgs),
        pos,
        [
            (piece, (rows, width), lambda r, pos, place=place: (place, 0))
            for piece, place in zip(pieces, places)
        ],
        [out_by_rel(groups, len(pieces) // 2 * msgs, width, BF)],
        grid=(groups,),
        after=after,
        limit=24,
    )[0]


def bases(pos, batch):
    half = batch // 2
    for core in (pos[3], 1 - pos[3]):
        for depth in LINE:
            owner = (pos[0] ^ depth) * SIDE * SIDE + pos[1] * SIDE + pos[2]
            yield owner * batch + core * half


def aggregate_part(scale, pos, batch, payloads, moved, side):
    rel = pl.program_id(0)
    half = batch // 2
    msgs = moved.shape[0] // len(payloads)
    dst = []
    for ref in payloads:
        owner, row, _, _ = fields(ref[ref.shape[0] - EXTRA :, :].astype(F32), rel, msgs)
        dst.append(owner * batch + row)
    dst = jnp.concatenate(dst, axis=1)
    rows = lax.broadcasted_iota(jnp.int32, (half, dst.shape[1]), 0)
    places = list(bases(pos, batch))[side * DEPTH : (side + 1) * DEPTH]
    hot = [one_hot(dst - base, rows) for base in places]
    return scale * dot(jnp.concatenate(hot, axis=0), moved)


def aggregate_near_kernel(scale, pos, own, near_a, near_b, one, two, mean, result):
    batch = mean.shape[1]
    half = batch // 2
    moved = jnp.concatenate([one[0], two[0]], axis=0)
    for side in range(2):
        total = aggregate_part(scale, pos, batch, [own, near_a, near_b], moved, side)
        core = pos[3] if side == 0 else 1 - pos[3]
        own_mean = mean[0, pl.ds(pl.multiple_of(core * half, half), half), :].astype(F32)
        at = side * DEPTH * half
        result[0, at : at + half, :] = total[:half] + own_mean
        result[0, at + half : at + DEPTH * half, :] = total[half:]


def aggregate_near(pos, mean, payloads, moved, scale, after):
    groups, batch, width = mean.shape
    return call(
        "aggregate_near",
        functools.partial(aggregate_near_kernel, scale),
        pos,
        [full(p) for p in payloads] + [by_rel(m) for m in moved] + [by_rel(mean)],
        [out_by_rel(groups, DEPTH * batch, width, F32)],
        grid=(groups,),
        after=after,
        limit=32,
    )[0]


def aggregate_kernel(scale, msgs, batch, pos, near_ab, far_ab, before, result):
    moved = gather_step(pos, pl.program_id(0), msgs, near_ab, far_ab)
    rows = DEPTH * batch // 2
    for side in range(2):
        span = slice(side * rows, (side + 1) * rows)
        total = aggregate_part(scale, pos, batch, [near_ab], moved, side)
        result[0, span, :] = (total + before[0, span, :]).astype(BF)


def aggregate(pos, msgs, batch, near_ab, far_ab, before, scale, after):
    groups, rows, width = before.shape
    return call(
        "aggregate",
        functools.partial(aggregate_kernel, scale, msgs, batch),
        pos,
        [full(near_ab), full(far_ab), by_rel(before)],
        [out_by_rel(groups, rows, width, BF)],
        grid=(groups,),
        after=after,
        limit=32,
    )[0]


def output_kernel(pos, sums, weight, result):
    total = dot(sums[0], weight[0])
    for rel in range(1, sums.shape[0]):
        total = total + dot(sums[rel], weight[rel])
    result[...] = total.astype(result.dtype)


def output_terms(pos, sums, weights, side, dtype, after):
    groups, rows, width = sums.shape
    return call(
        "output_terms",
        output_kernel,
        pos,
        [(sums, (groups, rows // 2, width), lambda s, pos: (0, side, 0)), full(weights)],
        [out((rows // 2, width), dtype)],
        after=after,
        limit=24,
    )[0]


def back_kernel(scale, batch, msgs, pos, payload, line, far, weight, kept, away, total):
    rel = pl.program_id(0)
    half = line.shape[0] // DEPTH
    owner, row, low, high = fields(
        payload[payload.shape[0] - EXTRA :, :].astype(F32), rel, msgs
    )
    column = jnp.transpose(jnp.broadcast_to(owner * batch + row, (128, msgs)))
    lanes = lax.broadcasted_iota(jnp.int32, (msgs, half), 1)
    hot = [one_hot(column, lanes + base) for base in bases(pos, batch)]
    picked = dot(jnp.concatenate(hot[:DEPTH], axis=1), line[...])
    picked = picked + dot(jnp.concatenate(hot[DEPTH:], axis=1), far[...])
    grads = (scale * dot(picked.astype(BF), weight[0], ((1,), (1,)))).astype(BF)
    rows = lax.broadcasted_iota(jnp.int32, (total.shape[0], msgs), 0)
    term = dot(one_hot(low + PART * high, rows), grads)

    @pl.when(rel == 0)
    def _():
        total[...] = term

    @pl.when(rel > 0)
    def _():
        total[...] += term

    @pl.when(rel == pl.num_programs(0) - 1)
    def _():
        size = kept.shape[0]
        kept[...] = total[pl.ds(pl.multiple_of(pos[3] * size, size), size), :]
        away[...] = total[pl.ds(pl.multiple_of((1 - pos[3]) * size, size), size), :].astype(BF)


def back_terms(pos, batch, msgs, payload, line, far, weights, scale, after):
    groups, width, _ = weights.shape
    half = payload.shape[0] - EXTRA
    return call(
        "feature_terms",
        functools.partial(back_kernel, scale, batch, msgs),
        pos,
        [full(payload), full(line), full(far), by_rel(weights)],
        [out((half, width), F32), out((half, width), BF)],
        grid=(groups,),
        after=after,
        scratch=[pltpu.VMEM((2 * half, width), F32)],
        limit=24,
    )


def sum_kernel(pos, *refs):
    total = refs[0][...].astype(F32)
    for ref in refs[1:-1]:
        total = total + ref[...].astype(F32)
    refs[-1][...] = total.astype(refs[-1].dtype)


def sum_rows_job(terms, dtype):
    shape = terms[0][0].shape
    ins = [(array, shape, lambda s, pos, place=place: (place, 0)) for array, place in terms]
    return (sum_kernel, ins, [out(shape, dtype)], {})


def sum_pair_kernel(pos, one, two, came, result):
    rows = one.shape[0]
    result[:rows, :] = (one[...] + came[:rows, :].astype(F32)).astype(BF)
    result[rows:, :] = (two[...] + came[rows:, :].astype(F32)).astype(BF)


def sum_pair_job(one, two, came):
    return (sum_pair_kernel, [full(one), full(two), full(came)], [out(came.shape, BF)], {})


def rows_fold_kernel(pos, kept, came, stay, away):
    rows = stay.shape[0]
    for ref, span in ((stay, slice(0, rows)), (away, slice(rows, 2 * rows))):
        ref[...] = (kept[span, :] + came[span, :].astype(F32)).astype(ref.dtype)


def rows_fold_job(kept, came):
    shape = (kept.shape[0] // 2, kept.shape[1])
    return (rows_fold_kernel, [full(kept), full(came)], [out(shape, F32), out(shape, BF)], {})


def line_sum_job(kept, came):
    return (sum_kernel, [full(kept), full(came)], [out(kept.shape, BF)], {})


def finish_kernel(pos, total, opposite, result):
    half = total.shape[0]
    result[pl.ds(pl.multiple_of(pos[3] * half, half), half), :] = total[...]
    result[pl.ds(pl.multiple_of((1 - pos[3]) * half, half), half), :] = opposite[...]


def finish_job(total, opposite):
    shape = (total.shape[0] * 2, total.shape[1])
    return (finish_kernel, [full(total), full(opposite)], [out(shape, BF)], {})


def weight_kernel(norm, sent, pos, sums, line, far, result):
    half = sums.shape[2] // 2
    rows = line.shape[0]
    place = jnp.where(pos[3] == 0, pos[1], pos[2])
    columns = pl.ds(pl.multiple_of((1 - place if sent else place) * half, 128), half)
    total = dot(sums[0, :rows, columns], line[...], ((0,), (0,)))
    total = total + dot(sums[0, rows:, columns], far[...], ((0,), (0,)))
    result[0] = (norm * total).astype(result.dtype)


def weight_terms(pos, sums, line, far, chunk, norm, sent, after):
    groups, _, width = sums.shape
    span = width // CHUNKS
    shape = (groups, width // 2, span)
    flat = lambda array: (array, (array.shape[0], span), lambda s, pos: (0, chunk))
    return call(
        "weight_terms",
        functools.partial(weight_kernel, norm, sent),
        pos,
        [by_rel(sums), flat(line), flat(far)],
        [(shape, BF if sent else F32, (1,) + shape[1:], lambda s, pos: (s, 0, 0))],
        grid=(groups,),
        after=after,
        limit=24,
    )[0]


PLACES = (
    lambda pos: jnp.where(pos[3] == 0, pos[2], pos[1]),
    lambda pos: pos[0] % 2,
)


def weight_fold_kernel(place, pos, kept, came, stay, away):
    rows = stay.shape[1]
    for ref, index in ((stay, place(pos)), (away, 1 - place(pos))):
        span = pl.ds(pl.multiple_of(index * rows, 16), rows)
        ref[...] = (kept[:, span, :] + came[:, span, :].astype(F32)).astype(ref.dtype)


def weight_fold_job(kept, came, place):
    shape = (kept.shape[0], kept.shape[1] // 2, kept.shape[2])
    return (
        functools.partial(weight_fold_kernel, place),
        [full(kept), full(came)],
        [out(shape, F32), out(shape, BF)],
        {},
    )


def assemble_kernel(pos, *refs):
    result = refs[-1]
    z, y, x, core = pos[0], pos[1], pos[2], pos[3]
    first = jnp.where(core == 0, y, x)
    second = jnp.where(core == 0, x, y)
    count = pl.num_programs(0)
    rows = result.shape[1] // (2 * SIDE * SIDE)
    for number, ref in enumerate(refs[:-1]):
        chunk, flip_a = number // 2, number % 2
        span = ref.shape[1]
        for index in range(4):
            flip_b, flip_z = index // 2, index % 2
            place = ((first ^ flip_a) * 2 + (second ^ flip_b)) * 2 + (z % 2 ^ flip_z)
            start = (index * count + pl.program_id(0)) * rows
            result[
                0, pl.ds(pl.multiple_of(place * rows, 16), rows), chunk * span : (chunk + 1) * span
            ] = ref[pl.ds(pl.multiple_of(start, 16), rows), :].astype(F32)


def assemble(pos, pieces, groups, width):
    return call(
        "assemble",
        assemble_kernel,
        pos,
        [full(piece) for piece in pieces],
        [out_by_rel(groups, width, width, F32)],
        grid=(groups,),
        limit=24,
    )[0]


def body(
    features, history, history_mean, weights, source_rows, target_owner, target_rows, cotangent
):
    groups, width, _ = weights.shape
    batch = history_mean.shape[1]
    nodes = features.shape[0]
    msgs = source_rows.shape[1]
    owners = lax.axis_size("node")
    scale = 1.0 / (msgs // batch)
    dst = target_owner[:, :, 0] * batch + target_rows
    if owners != NODES_HERE:
        return anywhere(
            features, history, history_mean, weights, source_rows, dst, cotangent, scale
        )
    norm = (batch * owners) ** -0.5
    node = lax.axis_index("node")
    core = lax.axis_index("rel")
    z = node // 4
    pos = jnp.stack([z, node // 2 % 2, node % 2, core]).astype(jnp.int32)
    half = batch // 2
    swap = lambda array: hop(array, CORES)
    numbers = jnp.stack(
        [target_owner[:, :, 0], target_rows, source_rows % PART, source_rows // PART], axis=1
    )
    numbers = numbers.reshape(groups * FIELDS, msgs).astype(BF)
    numbers = jnp.concatenate([numbers, jnp.zeros((EXTRA - groups * FIELDS, msgs), BF)])

    own, theirs, mine = prepare(pos, features, history, numbers, cotangent)
    near_a, near_b = hop(own, FIRST), hop(own, SECOND)
    line_2 = hop(mine, ALONG[2])
    collect = functools.partial(gather, pos, groups, msgs)
    one = collect([own, theirs], [0, 0], [mine])
    (near,), (pair,), (near_b,) = together(
        pos, [join_job([near_a, near_b]), join_job([mine, line_2]), (copy_kernel, [full(near_b)], [out(near_b.shape, BF)], {})], [one]
    )
    near_ab, near_o, line_1 = hop(near_b, FIRST), swap(near), hop(pair, ALONG[1])
    two = collect([near_a, near_o, near_b, near_o], [0, 1, 0, 0], [near_b])
    ((near_ab,),) = together(pos, [gate_job([near_ab])], [two])
    far_ab = swap(near_ab)
    sums = aggregate_near(
        pos, history_mean, [own, near_a, near_b], [one, two], scale, [near_ab]
    )
    ((line,),) = together(pos, [join_job([pair, line_1])], [sums, far_ab])
    far = swap(line)
    sums = aggregate(pos, msgs, batch, near_ab, far_ab, sums, scale, [line])
    plane = [own, near_a, near_b, near_ab]

    chunks = [{"index": index} for index in range(CHUNKS)]
    last = sums
    for chunk in chunks:
        last = weight_terms(pos, sums, line, far, chunk["index"], norm, True, [last])
        chunk["came"] = hop(last, FIRST)
        if chunk["index"] == 0:
            theirs = output_terms(pos, sums, weights, 1, BF, [last])
            last = output = output_terms(pos, sums, weights, 0, F32, [theirs])
    for chunk in chunks:
        last = weight_terms(pos, sums, line, far, chunk["index"], norm, False, [last])
        chunk["kept"] = last
    state, grown, given = {"away": theirs, "kept": output}, {}, {}
    ways = (SECOND, ALONG[1], ALONG[2])

    def weight_step(chunk, step):
        if step < 2:

            def sent(kept, away):
                chunk["kept"], chunk["came"] = kept, hop(away, ways[step])

            return weight_fold_job(chunk["kept"], chunk["came"], PLACES[step]), sent
        if step == 2:
            def exchanged(total):
                chunk["kept"], chunk["came"] = total, hop(total, ALONG[2])

            return line_sum_job(chunk["kept"], chunk["came"]), exchanged
        if step == 3:

            def summed(total):
                total = total.reshape(-1, total.shape[2])
                chunk["line"] = [total, hop(total, ALONG[1])]

            return line_sum_job(chunk["kept"], chunk["came"]), summed

        def joined(line):
            chunk["line"] = [line, hop(line, (SECOND, FIRST)[step - 4])]

        return join_job(chunk["line"]), joined

    def rows_step(step):
        if step == 0:
            return gate_job([state["away"]]), lambda away: state.update(rows=swap(away))
        if step < 3:

            def sent(kept, away):
                state.update(kept=kept, rows=hop(away, ways[step]))

            return rows_fold_job(state["kept"], state["rows"]), sent
        if step == 3:
            job = line_sum_job(state["kept"], state["rows"])
            return job, lambda total: state.update(total=total, opposite=swap(total))
        job = finish_job(state["total"], state["opposite"])
        return job, lambda rows: state.update(out=rows)

    def back_step(step):
        if step == 0:
            job = join_job([given[2], given[3]])
            return job, lambda away: state.update(far=swap(away))
        if step == 1:
            return gate_job([given[1]]), lambda away: state.update(far_2=swap(away))
        if step == 2:
            job = sum_pair_job(grown[1], grown[3], state["far"])
            return job, lambda away: state.update(first=hop(away, FIRST))
        if step == 3:
            job = sum_rows_job([(grown[2], 0), (state["far_2"], 0), (state["first"], 1)], BF)
            return job, lambda away: state.update(second=hop(away, SECOND))
        if step == 4:
            return gate_job([given[0]]), lambda away: state.update(far_0=swap(away))
        if step == 5:
            terms = [(grown[0], 0), (state["far_0"], 0), (state["first"], 0), (state["second"], 0)]
            job = sum_rows_job(terms, BF)
            return job, lambda own: state.update(own=own, own_o=swap(own))
        job = finish_job(state["own"], state["own_o"])
        return job, lambda rows: state.update(back=rows)

    for steps, covers in ROUNDS:
        planned = []
        for what, step in steps:
            if what == "rows":
                planned.append(rows_step(step))
            elif what == "back":
                planned.append(back_step(step))
            else:
                planned.append(weight_step(chunks[what], step))
        results = together(pos, [job for job, _ in planned], [last])
        for (_, then), result in zip(planned, results):
            then(*result)
        last = results[0][0]
        for cover in covers:
            grown[cover], given[cover] = back_terms(
                pos, batch, msgs, plane[cover], line, far, weights, scale, [last]
            )
            last = grown[cover]
    pieces = [piece for chunk in chunks for piece in chunk["line"]]
    return state["out"], assemble(pos, pieces, groups, width), state["back"]


def anywhere(features, history, history_mean, weights, source_rows, dst, cotangent, scale):
    groups, width, _ = weights.shape
    batch, nodes = cotangent.shape[0], features.shape[0]
    total_batch = batch * lax.axis_size("node")
    deltas = (features.astype(F32) - history.astype(F32)).astype(BF)
    every = lax.all_gather(cotangent, "node", tiled=True)
    out = jnp.zeros((total_batch, width), F32)
    local = jnp.zeros((batch, width), F32)
    terms = jnp.zeros((nodes, width), F32)
    grads = []
    for rel in range(groups):
        rows = jnp.take(deltas, source_rows[rel], axis=0)
        picked = jnp.take(every, dst[rel], axis=0)
        out = out.at[dst[rel]].add(scale * dot(rows, weights[rel]))
        local = local + dot(history_mean[rel], weights[rel])
        edge = (scale * dot(picked, weights[rel], ((1,), (1,)))).astype(BF)
        terms = terms.at[source_rows[rel]].add(edge.astype(F32))
        grads.append(
            dot(history_mean[rel], cotangent, ((0,), (0,)))
            + scale * dot(rows, picked, ((0,), (0,)))
        )
    layer_out = lax.psum(lax.psum_scatter(out, "node", tiled=True) + local, "rel").astype(BF)
    weight_grads = lax.psum(jnp.stack(grads) * total_batch**-0.5, "node")
    return layer_out, weight_grads, lax.psum(terms, "rel").astype(BF)


def solution(mesh):
    in_specs = (
        P("node", None),
        P("node", None),
        P("rel", "node", None),
        P("rel", None, None),
        P("rel", "node"),
        P("rel", "node", None),
        P("rel", "node"),
        P("node", None),
    )
    out_specs = (P("node", None), P("rel", None, None), P("node", None))
    return jax.shard_map(body, mesh=mesh, in_specs=in_specs, out_specs=out_specs, check_vma=False)
```

```python
import functools

import jax
import jax.numpy as jnp
from jax import lax
from jax.experimental import pallas as pl
from jax.experimental.pallas import tpu as pltpu
from jax.sharding import PartitionSpec as P

BF = jnp.bfloat16
F32 = jnp.float32
AXES = ("node", "rel")
DEPTH, SIDE = 4, 2
CHUNKS = 2
LIMIT = 12
ROUNDS = (
    (((0, 0),), (2,)),
    (((1, 0), (0, 1),), (3,)),
    (((0, 2), (1, 1), ("back", 0), ("rows", 0),), (1,)),
    (((0, 3), (1, 2), ("back", 2), ("back", 1),), (0,)),
    (((0, 4), (1, 3), ("back", 3), ("back", 4), ("rows", 1),), ()),
    (((0, 5), (1, 4), ("back", 5),), ()),
    (((1, 5), ("back", 6), ("rows", 2),), ()),
    ((("rows", 3),), ()),
    ((("rows", 4),), ()),
)
NODES_HERE = DEPTH * SIDE * SIDE


def dot(a, b, dims=((1,), (0,))):
    return lax.dot_general(a, b, (dims, ((), ())), preferred_element_type=F32)


def call(name, kernel, pos, ins, outs, grid=(1,), after=(), alias=None, limit=24, scratch=()):
    def spec(block, index):
        if block is None:
            return pl.BlockSpec(memory_space=pl.ANY)
        if index is None:
            return pl.BlockSpec(block, lambda *_: (0,) * len(block))
        return pl.BlockSpec(block, index)

    many = len(ins)

    def run(pos_ref, *refs):
        kernel(pos_ref, *refs[:many], *refs[many + len(after) :])

    return pl.pallas_call(
        run,
        grid_spec=pltpu.PrefetchScalarGridSpec(
            num_scalar_prefetch=1,
            grid=grid,
            in_specs=[spec(block, index) for _, block, index in ins]
            + [pl.BlockSpec(memory_space=pl.ANY)] * len(after),
            out_specs=[spec(block, index) for _, _, block, index in outs],
            scratch_shapes=scratch,
        ),
        out_shape=[jax.ShapeDtypeStruct(shape, dtype) for shape, dtype, _, _ in outs],
        input_output_aliases=alias or {},
        compiler_params=pltpu.CompilerParams(
            dimension_semantics=("arbitrary",) * len(grid), vmem_limit_bytes=limit * 1024 * 1024
        ),
        cost_estimate=pl.CostEstimate(flops=1000, bytes_accessed=1000, transcendentals=0),
        name=name,
    )(pos, *[array for array, _, _ in ins], *after)


def full(array):
    return (array, array.shape, None)


def out(shape, dtype):
    return (shape, dtype, shape, None)


def together(pos, jobs, after):
    ins = [entry for _, job_ins, _, _ in jobs for entry in job_ins]
    outs = [entry for _, _, job_outs, _ in jobs for entry in job_outs]
    spans, alias, i, o = [], {}, 0, 0
    for _, job_ins, job_outs, job_alias in jobs:
        spans.append((i, i + len(job_ins), o, o + len(job_outs)))
        alias.update({1 + i + source: o + target for source, target in job_alias.items()})
        i, o = spans[-1][1], spans[-1][3]

    def kernel(pos_ref, *refs):
        for (work, _, _, _), (a, b, c, d) in zip(jobs, spans):
            work(pos_ref, *refs[a:b], *refs[len(ins) + c : len(ins) + d])

    results = call("step", kernel, pos, ins, outs, after=after, alias=alias, limit=LIMIT)
    return [results[c:d] for _, _, c, d in spans]


def gate_job(arrays):
    return (
        lambda *_: None,
        [(array, None, None) for array in arrays],
        [(array.shape, array.dtype, None, None) for array in arrays],
        {i: i for i in range(len(arrays))},
    )


def pairs(move):
    listed = []
    for node in range(NODES_HERE):
        for core in range(2):
            z, y, x = node // 4, node // 2 % 2, node % 2
            tz, ty, tx, tc = move(z, y, x, core)
            listed.append((node * 2 + core, (tz * 4 + ty * 2 + tx) * 2 + tc))
    return listed


FIRST = pairs(lambda z, y, x, c: (z, y ^ (1 - c), x ^ c, c))
SECOND = pairs(lambda z, y, x, c: (z, y ^ c, x ^ (1 - c), c))
ALONG = [pairs(lambda z, y, x, c, k=k: (z ^ k, y, x, c)) for k in range(DEPTH)]
LINE = (0, 2, 1, 3)
CORES = pairs(lambda z, y, x, c: (z, y, x, 1 - c))


def hop(array, table):
    return lax.ppermute(array, AXES, table)


def by_rel(array):
    return (array, (1,) + array.shape[1:], lambda r, pos: (r, 0, 0))


def out_by_rel(groups, rows, width, dtype):
    return ((groups, rows, width), dtype, (1, rows, width), lambda r, pos: (r, 0, 0))


def join_kernel(pos, *refs):
    start = 0
    for ref in refs[:-1]:
        refs[-1][start : start + ref.shape[0], :] = ref[...]
        start += ref.shape[0]


def copy_kernel(pos, source, target):
    target[...] = source[...]


def join_job(pieces):
    shape = (sum(piece.shape[0] for piece in pieces), pieces[0].shape[1])
    return (join_kernel, [full(piece) for piece in pieces], [out(shape, BF)], {})


def one_hot(values, places):
    return (values == places).astype(F32).astype(BF)


def partial_step(pos, core, first, second, batch, dst, sent, local):
    half = batch // 2
    rows = lax.broadcasted_iota(jnp.int32, (half, dst.shape[1]), 0)
    hot = []
    for depth in LINE:
        base = owner_of(pos, core, first, second, depth) * batch + core * half
        hot.append(one_hot(dst[...] - base, rows))
    total = dot(jnp.concatenate(hot, axis=0), sent[...])
    own = local[pl.ds(pl.multiple_of(core * half, half), half), :]
    here = (first + second == 0).astype(F32)
    return jnp.concatenate([total[:half] + here * own, total[half:]], axis=0)


def one_hot(values, places):
    return (values == places).astype(F32).astype(BF)


FIELDS = 4
EXTRA = 16
PART = 256


def fields(block, rel, count):
    places = lax.broadcasted_iota(jnp.int32, block.shape, 0)
    rows = [
        jnp.sum(jnp.where(places == rel * FIELDS + f, block, 0.0), axis=0, keepdims=True)
        for f in range(FIELDS)
    ]
    return [row[:, :count].astype(jnp.int32) for row in rows]


def prepare_kernel(pos, feat, hist, numbers, cot, mine, theirs, line):
    half = feat.shape[0] // 2
    for ref, core in ((mine, pos[3]), (theirs, 1 - pos[3])):
        span = pl.ds(pl.multiple_of(core * half, half), half)
        deltas = feat[span, :].astype(F32) - hist[span, :].astype(F32)
        ref[:half, :] = deltas.astype(BF)
        ref[half:, :] = jnp.zeros((EXTRA, ref.shape[1]), BF)
        ref[half:, : numbers.shape[1]] = numbers[...]
    half = line.shape[0]
    line[...] = cot[pl.ds(pl.multiple_of(pos[3] * half, half), half), :]


def prepare(pos, features, history, numbers, cot):
    nodes, width = features.shape
    shape = (nodes // 2 + EXTRA, width)
    return call(
        "prepare",
        prepare_kernel,
        pos,
        [full(features), full(history), full(numbers), full(cot)],
        [out(shape, BF), out(shape, BF), out((cot.shape[0] // 2, width), BF)],
        limit=24,
    )


def gather_step(pos, rel, msgs, mine, theirs):
    half = mine.shape[0] - EXTRA
    _, _, low, high = fields(mine[half:, :].astype(F32), rel, msgs)
    column = jnp.transpose(jnp.broadcast_to(low + PART * high, (128, msgs)))
    lanes = lax.broadcasted_iota(jnp.int32, (msgs, 128), 1)
    total = None
    for ref, core in ((mine, pos[3]), (theirs, 1 - pos[3])):
        hot = [one_hot(column, lanes + (core * half + n)) for n in range(0, half, 128)]
        term = dot(jnp.concatenate(hot, axis=1), ref[:half, :])
        total = term if total is None else total + term
    return total.astype(BF)


def gather_kernel(msgs, pos, *refs):
    result = refs[-1]
    for n in range(len(refs) // 2):
        result[0, n * msgs : (n + 1) * msgs, :] = gather_step(
            pos, pl.program_id(0), msgs, refs[2 * n], refs[2 * n + 1]
        )


def gather(pos, groups, msgs, pieces, places, after):
    rows, width = pieces[0].shape
    return call(
        "gather",
        functools.partial(gather_kernel, msgs),
        pos,
        [
            (piece, (rows, width), lambda r, pos, place=place: (place, 0))
            for piece, place in zip(pieces, places)
        ],
        [out_by_rel(groups, len(pieces) // 2 * msgs, width, BF)],
        grid=(groups,),
        after=after,
        limit=24,
    )[0]


def bases(pos, batch):
    half = batch // 2
    for core in (pos[3], 1 - pos[3]):
        for depth in LINE:
            owner = (pos[0] ^ depth) * SIDE * SIDE + pos[1] * SIDE + pos[2]
            yield owner * batch + core * half


def aggregate_part(scale, pos, batch, payloads, moved, side):
    rel = pl.program_id(0)
    half = batch // 2
    msgs = moved.shape[0] // len(payloads)
    dst = []
    for ref in payloads:
        owner, row, _, _ = fields(ref[ref.shape[0] - EXTRA :, :].astype(F32), rel, msgs)
        dst.append(owner * batch + row)
    dst = jnp.concatenate(dst, axis=1)
    rows = lax.broadcasted_iota(jnp.int32, (half, dst.shape[1]), 0)
    places = list(bases(pos, batch))[side * DEPTH : (side + 1) * DEPTH]
    hot = [one_hot(dst - base, rows) for base in places]
    return scale * dot(jnp.concatenate(hot, axis=0), moved)


def aggregate_near_kernel(scale, pos, own, near_a, near_b, one, two, mean, result):
    batch = mean.shape[1]
    half = batch // 2
    moved = jnp.concatenate([one[0], two[0]], axis=0)
    for side in range(2):
        total = aggregate_part(scale, pos, batch, [own, near_a, near_b], moved, side)
        core = pos[3] if side == 0 else 1 - pos[3]
        own_mean = mean[0, pl.ds(pl.multiple_of(core * half, half), half), :].astype(F32)
        at = side * DEPTH * half
        result[0, at : at + half, :] = total[:half] + own_mean
        result[0, at + half : at + DEPTH * half, :] = total[half:]


def aggregate_near(pos, mean, payloads, moved, scale, after):
    groups, batch, width = mean.shape
    return call(
        "aggregate_near",
        functools.partial(aggregate_near_kernel, scale),
        pos,
        [full(p) for p in payloads] + [by_rel(m) for m in moved] + [by_rel(mean)],
        [out_by_rel(groups, DEPTH * batch, width, F32)],
        grid=(groups,),
        after=after,
        limit=32,
    )[0]


def aggregate_kernel(scale, msgs, batch, pos, near_ab, far_ab, before, result):
    moved = gather_step(pos, pl.program_id(0), msgs, near_ab, far_ab)
    rows = DEPTH * batch // 2
    for side in range(2):
        span = slice(side * rows, (side + 1) * rows)
        total = aggregate_part(scale, pos, batch, [near_ab], moved, side)
        result[0, span, :] = (total + before[0, span, :]).astype(BF)


def aggregate(pos, msgs, batch, near_ab, far_ab, before, scale, after):
    groups, rows, width = before.shape
    return call(
        "aggregate",
        functools.partial(aggregate_kernel, scale, msgs, batch),
        pos,
        [full(near_ab), full(far_ab), by_rel(before)],
        [out_by_rel(groups, rows, width, BF)],
        grid=(groups,),
        after=after,
        limit=32,
    )[0]


def output_kernel(pos, sums, weight, result):
    total = dot(sums[0], weight[0])
    for rel in range(1, sums.shape[0]):
        total = total + dot(sums[rel], weight[rel])
    result[...] = total.astype(result.dtype)


def output_terms(pos, sums, weights, side, dtype, after):
    groups, rows, width = sums.shape
    return call(
        "output_terms",
        output_kernel,
        pos,
        [(sums, (groups, rows // 2, width), lambda s, pos: (0, side, 0)), full(weights)],
        [out((rows // 2, width), dtype)],
        after=after,
        limit=24,
    )[0]


def back_kernel(scale, batch, msgs, pos, payload, line, far, weight, kept, away, total):
    rel = pl.program_id(0)
    half = line.shape[0] // DEPTH
    owner, row, low, high = fields(
        payload[payload.shape[0] - EXTRA :, :].astype(F32), rel, msgs
    )
    column = jnp.transpose(jnp.broadcast_to(owner * batch + row, (128, msgs)))
    lanes = lax.broadcasted_iota(jnp.int32, (msgs, half), 1)
    hot = [one_hot(column, lanes + base) for base in bases(pos, batch)]
    picked = dot(jnp.concatenate(hot[:DEPTH], axis=1), line[...])
    picked = picked + dot(jnp.concatenate(hot[DEPTH:], axis=1), far[...])
    grads = (scale * dot(picked.astype(BF), weight[0], ((1,), (1,)))).astype(BF)
    rows = lax.broadcasted_iota(jnp.int32, (total.shape[0], msgs), 0)
    term = dot(one_hot(low + PART * high, rows), grads)

    @pl.when(rel == 0)
    def _():
        total[...] = term

    @pl.when(rel > 0)
    def _():
        total[...] += term

    @pl.when(rel == pl.num_programs(0) - 1)
    def _():
        size = kept.shape[0]
        kept[...] = total[pl.ds(pl.multiple_of(pos[3] * size, size), size), :]
        away[...] = total[pl.ds(pl.multiple_of((1 - pos[3]) * size, size), size), :].astype(BF)


def back_terms(pos, batch, msgs, payload, line, far, weights, scale, after):
    groups, width, _ = weights.shape
    half = payload.shape[0] - EXTRA
    return call(
        "feature_terms",
        functools.partial(back_kernel, scale, batch, msgs),
        pos,
        [full(payload), full(line), full(far), by_rel(weights)],
        [out((half, width), F32), out((half, width), BF)],
        grid=(groups,),
        after=after,
        scratch=[pltpu.VMEM((2 * half, width), F32)],
        limit=24,
    )


def sum_kernel(pos, *refs):
    total = refs[0][...].astype(F32)
    for ref in refs[1:-1]:
        total = total + ref[...].astype(F32)
    refs[-1][...] = total.astype(refs[-1].dtype)


def sum_rows_job(terms, dtype):
    shape = terms[0][0].shape
    ins = [(array, shape, lambda s, pos, place=place: (place, 0)) for array, place in terms]
    return (sum_kernel, ins, [out(shape, dtype)], {})


def sum_pair_kernel(pos, one, two, came, result):
    rows = one.shape[0]
    result[:rows, :] = (one[...] + came[:rows, :].astype(F32)).astype(BF)
    result[rows:, :] = (two[...] + came[rows:, :].astype(F32)).astype(BF)


def sum_pair_job(one, two, came):
    return (sum_pair_kernel, [full(one), full(two), full(came)], [out(came.shape, BF)], {})


def rows_fold_kernel(pos, kept, came, stay, away):
    rows = stay.shape[0]
    for ref, span in ((stay, slice(0, rows)), (away, slice(rows, 2 * rows))):
        ref[...] = (kept[span, :] + came[span, :].astype(F32)).astype(ref.dtype)


def rows_fold_job(kept, came):
    shape = (kept.shape[0] // 2, kept.shape[1])
    return (rows_fold_kernel, [full(kept), full(came)], [out(shape, F32), out(shape, BF)], {})


def line_sum_job(kept, came):
    return (sum_kernel, [full(kept), full(came)], [out(kept.shape, BF)], {})


def finish_kernel(pos, total, opposite, result):
    half = total.shape[0]
    result[pl.ds(pl.multiple_of(pos[3] * half, half), half), :] = total[...]
    result[pl.ds(pl.multiple_of((1 - pos[3]) * half, half), half), :] = opposite[...]


def finish_job(total, opposite):
    shape = (total.shape[0] * 2, total.shape[1])
    return (finish_kernel, [full(total), full(opposite)], [out(shape, BF)], {})


def weight_kernel(norm, sent, pos, sums, line, far, result):
    half = sums.shape[2] // 2
    rows = line.shape[0]
    place = jnp.where(pos[3] == 0, pos[1], pos[2])
    columns = pl.ds(pl.multiple_of((1 - place if sent else place) * half, 128), half)
    total = dot(sums[0, :rows, columns], line[...], ((0,), (0,)))
    total = total + dot(sums[0, rows:, columns], far[...], ((0,), (0,)))
    result[0] = (norm * total).astype(result.dtype)


def weight_terms(pos, sums, line, far, chunk, norm, sent, after):
    groups, _, width = sums.shape
    span = width // CHUNKS
    shape = (groups, width // 2, span)
    flat = lambda array: (array, (array.shape[0], span), lambda s, pos: (0, chunk))
    return call(
        "weight_terms",
        functools.partial(weight_kernel, norm, sent),
        pos,
        [by_rel(sums), flat(line), flat(far)],
        [(shape, BF if sent else F32, (1,) + shape[1:], lambda s, pos: (s, 0, 0))],
        grid=(groups,),
        after=after,
        limit=24,
    )[0]


PLACES = (
    lambda pos: jnp.where(pos[3] == 0, pos[2], pos[1]),
    lambda pos: pos[0] % 2,
)


def weight_fold_kernel(place, pos, kept, came, stay, away):
    rows = stay.shape[1]
    for ref, index in ((stay, place(pos)), (away, 1 - place(pos))):
        span = pl.ds(pl.multiple_of(index * rows, 16), rows)
        ref[...] = (kept[:, span, :] + came[:, span, :].astype(F32)).astype(ref.dtype)


def weight_fold_job(kept, came, place):
    shape = (kept.shape[0], kept.shape[1] // 2, kept.shape[2])
    return (
        functools.partial(weight_fold_kernel, place),
        [full(kept), full(came)],
        [out(shape, F32), out(shape, BF)],
        {},
    )


def assemble_kernel(pos, *refs):
    result = refs[-1]
    second = jnp.where(pos[3] == 0, pos[2], pos[1])
    count = pl.num_programs(0)
    rows = result.shape[1] // (2 * SIDE)
    for flip_a in range(2):

        @pl.when(pl.program_id(1) == flip_a)
        def _():
            for chunk, ref in enumerate(refs[flip_a:-1:2]):
                span = ref.shape[1]
                for index in range(4):
                    flip_b, flip_z = index // 2, index % 2
                    place = (second ^ flip_b) * 2 + (pos[0] % 2 ^ flip_z)
                    start = (index * count + pl.program_id(0)) * rows
                    result[
                        0,
                        pl.ds(pl.multiple_of(place * rows, 16), rows),
                        chunk * span : (chunk + 1) * span,
                    ] = ref[pl.ds(pl.multiple_of(start, 16), rows), :].astype(F32)


def assemble(pos, pieces, groups, width):
    half = lambda r, f, pos: (r, jnp.where(pos[3] == 0, pos[1], pos[2]) ^ f, 0)
    return call(
        "assemble",
        assemble_kernel,
        pos,
        [full(piece) for piece in pieces],
        [((groups, width, width), F32, (1, width // 2, width), half)],
        grid=(groups, 2),
        limit=24,
    )[0]


def body(
    features, history, history_mean, weights, source_rows, target_owner, target_rows, cotangent
):
    groups, width, _ = weights.shape
    batch = history_mean.shape[1]
    nodes = features.shape[0]
    msgs = source_rows.shape[1]
    owners = lax.axis_size("node")
    scale = 1.0 / (msgs // batch)
    dst = target_owner[:, :, 0] * batch + target_rows
    if owners != NODES_HERE:
        return anywhere(
            features, history, history_mean, weights, source_rows, dst, cotangent, scale
        )
    norm = (batch * owners) ** -0.5
    node = lax.axis_index("node")
    core = lax.axis_index("rel")
    z = node // 4
    pos = jnp.stack([z, node // 2 % 2, node % 2, core]).astype(jnp.int32)
    half = batch // 2
    swap = lambda array: hop(array, CORES)
    numbers = jnp.stack(
        [target_owner[:, :, 0], target_rows, source_rows % PART, source_rows // PART], axis=1
    )
    numbers = numbers.reshape(groups * FIELDS, msgs).astype(BF)
    numbers = jnp.concatenate([numbers, jnp.zeros((EXTRA - groups * FIELDS, msgs), BF)])

    own, theirs, mine = prepare(pos, features, history, numbers, cotangent)
    near_a, near_b = hop(own, FIRST), hop(own, SECOND)
    line_2 = hop(mine, ALONG[2])
    collect = functools.partial(gather, pos, groups, msgs)
    one = collect([own, theirs], [0, 0], [mine])
    (near,), (pair,), (near_b,) = together(
        pos, [join_job([near_a, near_b]), join_job([mine, line_2]), (copy_kernel, [full(near_b)], [out(near_b.shape, BF)], {})], [one]
    )
    near_ab, near_o, line_1 = hop(near_b, FIRST), swap(near), hop(pair, ALONG[1])
    two = collect([near_a, near_o, near_b, near_o], [0, 1, 0, 0], [near_b])
    ((near_ab,),) = together(pos, [gate_job([near_ab])], [two])
    far_ab = swap(near_ab)
    sums = aggregate_near(
        pos, history_mean, [own, near_a, near_b], [one, two], scale, [near_ab]
    )
    ((line,),) = together(pos, [join_job([pair, line_1])], [sums, far_ab])
    far = swap(line)
    sums = aggregate(pos, msgs, batch, near_ab, far_ab, sums, scale, [line])
    plane = [own, near_a, near_b, near_ab]

    chunks = [{"index": index} for index in range(CHUNKS)]
    last = sums
    for chunk in chunks:
        last = weight_terms(pos, sums, line, far, chunk["index"], norm, True, [last])
        chunk["came"] = hop(last, FIRST)
        if chunk["index"] == 0:
            theirs = output_terms(pos, sums, weights, 1, BF, [last])
            last = output = output_terms(pos, sums, weights, 0, F32, [theirs])
    for chunk in chunks:
        last = weight_terms(pos, sums, line, far, chunk["index"], norm, False, [last])
        chunk["kept"] = last
    state, grown, given = {"away": theirs, "kept": output}, {}, {}
    ways = (SECOND, ALONG[1], ALONG[2])

    def weight_step(chunk, step):
        if step < 2:

            def sent(kept, away):
                chunk["kept"], chunk["came"] = kept, hop(away, ways[step])

            return weight_fold_job(chunk["kept"], chunk["came"], PLACES[step]), sent
        if step == 2:
            def exchanged(total):
                chunk["kept"], chunk["came"] = total, hop(total, ALONG[2])

            return line_sum_job(chunk["kept"], chunk["came"]), exchanged
        if step == 3:

            def summed(total):
                total = total.reshape(-1, total.shape[2])
                chunk["line"] = [total, hop(total, ALONG[1])]

            return line_sum_job(chunk["kept"], chunk["came"]), summed

        def joined(line):
            chunk["line"] = [line, hop(line, (SECOND, FIRST)[step - 4])]

        return join_job(chunk["line"]), joined

    def rows_step(step):
        if step == 0:
            return gate_job([state["away"]]), lambda away: state.update(rows=swap(away))
        if step < 3:

            def sent(kept, away):
                state.update(kept=kept, rows=hop(away, ways[step]))

            return rows_fold_job(state["kept"], state["rows"]), sent
        if step == 3:
            job = line_sum_job(state["kept"], state["rows"])
            return job, lambda total: state.update(total=total, opposite=swap(total))
        job = finish_job(state["total"], state["opposite"])
        return job, lambda rows: state.update(out=rows)

    def back_step(step):
        if step == 0:
            job = join_job([given[2], given[3]])
            return job, lambda away: state.update(far=swap(away))
        if step == 1:
            return gate_job([given[1]]), lambda away: state.update(far_2=swap(away))
        if step == 2:
            job = sum_pair_job(grown[1], grown[3], state["far"])
            return job, lambda away: state.update(first=hop(away, FIRST))
        if step == 3:
            job = sum_rows_job([(grown[2], 0), (state["far_2"], 0), (state["first"], 1)], BF)
            return job, lambda away: state.update(second=hop(away, SECOND))
        if step == 4:
            return gate_job([given[0]]), lambda away: state.update(far_0=swap(away))
        if step == 5:
            terms = [(grown[0], 0), (state["far_0"], 0), (state["first"], 0), (state["second"], 0)]
            job = sum_rows_job(terms, BF)
            return job, lambda own: state.update(own=own, own_o=swap(own))
        job = finish_job(state["own"], state["own_o"])
        return job, lambda rows: state.update(back=rows)

    for steps, covers in ROUNDS:
        planned = []
        for what, step in steps:
            if what == "rows":
                planned.append(rows_step(step))
            elif what == "back":
                planned.append(back_step(step))
            else:
                planned.append(weight_step(chunks[what], step))
        results = together(pos, [job for job, _ in planned], [last])
        for (_, then), result in zip(planned, results):
            then(*result)
        last = results[0][0]
        for cover in covers:
            grown[cover], given[cover] = back_terms(
                pos, batch, msgs, plane[cover], line, far, weights, scale, [last]
            )
            last = grown[cover]
    pieces = [piece for chunk in chunks for piece in chunk["line"]]
    return state["out"], assemble(pos, pieces, groups, width), state["back"]


def anywhere(features, history, history_mean, weights, source_rows, dst, cotangent, scale):
    groups, width, _ = weights.shape
    batch, nodes = cotangent.shape[0], features.shape[0]
    total_batch = batch * lax.axis_size("node")
    deltas = (features.astype(F32) - history.astype(F32)).astype(BF)
    every = lax.all_gather(cotangent, "node", tiled=True)
    out = jnp.zeros((total_batch, width), F32)
    local = jnp.zeros((batch, width), F32)
    terms = jnp.zeros((nodes, width), F32)
    grads = []
    for rel in range(groups):
        rows = jnp.take(deltas, source_rows[rel], axis=0)
        picked = jnp.take(every, dst[rel], axis=0)
        out = out.at[dst[rel]].add(scale * dot(rows, weights[rel]))
        local = local + dot(history_mean[rel], weights[rel])
        edge = (scale * dot(picked, weights[rel], ((1,), (1,)))).astype(BF)
        terms = terms.at[source_rows[rel]].add(edge.astype(F32))
        grads.append(
            dot(history_mean[rel], cotangent, ((0,), (0,)))
            + scale * dot(rows, picked, ((0,), (0,)))
        )
    layer_out = lax.psum(lax.psum_scatter(out, "node", tiled=True) + local, "rel").astype(BF)
    weight_grads = lax.psum(jnp.stack(grads) * total_batch**-0.5, "node")
    return layer_out, weight_grads, lax.psum(terms, "rel").astype(BF)


def solution(mesh):
    in_specs = (
        P("node", None),
        P("node", None),
        P("rel", "node", None),
        P("rel", None, None),
        P("rel", "node"),
        P("rel", "node", None),
        P("rel", "node"),
        P("node", None),
    )
    out_specs = (P("node", None), P("rel", None, None), P("node", None))
    return jax.shard_map(body, mesh=mesh, in_specs=in_specs, out_specs=out_specs, check_vma=False)
```
